256 devices in a mesh: level: 4 (over y), gx: 8 (over z_hi, core), gy: 8 (over x, z_lo).
Axes of the slice: x: 4, y: 4, z: 8 (z_hi: 4, z_lo: 2; z = z_hi * 2 + z_lo), core: 2. Of those that a mesh axis runs over, the one named last changes fastest.
Arguments:
- state_init: float32 [2, 128, 128, 128], P(None, 'gx', 'gy'), may hold values from 0 to 1
- feed_rate: float32 [128, 128, 128], P('gx', 'gy'), may hold values from 0.04 to 0.4
- kill_rate: float32 [128, 128, 128], P('gx', 'gy'), may hold values from 0.04 to 0.4
Outputs:
- level_states: float32 [4, 2, 128, 128, 128], P('level', None, 'gx', 'gy')
The draws below stay inside these ranges and needn't reach their ends.
All inputs are finite; a program needn't handle non-finite values.
Results may differ from the reference program's by a relative error of at most 0.00002.
Values sent between devices are 32-bit elements; how exact they have to be, the bound alone decides.
No kernel may reach another device: no remote copies, remote signals or barrier semaphores. Data moves between devices by JAX's collectives and lax.ppermute only.
A program may use at most 128 MiB of HBM per device.

```python
import math
import jax
import jax.numpy as jnp

NZ = 128
SWEEPS = 4
STEPS = 4
LEVELS = 4
NX = 128
NY = 128


def shard_levels(stream_key, dims, cuts, smallest, top_value):
    loudness = 1.0
    for position, shards_of in cuts:
        heights = jax.random.uniform(jax.random.fold_in(jax.random.fold_in(stream_key, 6), position), (shards_of,), jnp.float32, smallest / len(cuts), top_value / len(cuts))
        loudness = loudness * jnp.repeat(jnp.exp(heights), dims[position] // shards_of).reshape((-1,) + (1,) * (len(dims) - 1 - position))
    return loudness


def setup_inputs(seed: int = 0) -> dict:
    arg_keys = jax.random.split(jax.random.key(seed), 4)
    return {
        "state_init": jnp.clip(1.0 * jax.random.uniform(arg_keys[0], (2, NX, NY, NZ), jnp.float32) ** shard_levels(arg_keys[0], (2, NX, NY, NZ), ((1, 8), (2, 8)), -0.2, 0.2), 0.0, 1.0),
        "feed_rate": jnp.clip(jnp.exp(math.log(0.4) - 2.3025851 * jax.random.uniform(arg_keys[1], (NX, NY, NZ), jnp.float32) ** shard_levels(arg_keys[1], (NX, NY, NZ), ((0, 8), (1, 8)), -0.2, 0.2)), 0.04, 0.4),
        "kill_rate": jnp.clip(jnp.exp(math.log(0.4) - 2.3025851 * jax.random.uniform(arg_keys[2], (NX, NY, NZ), jnp.float32) ** shard_levels(arg_keys[2], (NX, NY, NZ), ((0, 8), (1, 8)), -0.2, 0.2)), 0.04, 0.4),
    }


STEP_H = 0.5


def quad_table(step_count):
    table_rows = []
    for n in range(step_count):
        first_node = min(max(n - 1, 0), step_count - 3)
        weights_row = []
        for j in range(4):
            coeffs = [1.0]
            for i in range(4):
                if i != j:
                    shifted = [0.0] + coeffs
                    scaled_terms = [-float(first_node + i) * c for c in coeffs] + [0.0]
                    coeffs = [(shifted[k] + scaled_terms[k]) / float(j - i) for k in range(len(shifted))]
            integral = 0.0
            for k in range(len(coeffs)):
                integral = integral + coeffs[k] * ((n + 1.0) ** (k + 1) - float(n) ** (k + 1)) / (k + 1.0)
            weights_row.append(integral)
        table_rows.append(weights_row)
    return table_rows


def diffuse_numbers():
    return jnp.array([0.5, 0.25], jnp.float32).reshape(2, 1, 1, 1)


def beside_sum(field):
    first = jnp.roll(field, -1, 1) + jnp.roll(field, 1, 1)
    second = jnp.roll(field, -1, 2) + jnp.roll(field, 1, 2)
    third = jnp.roll(field, -1, 3) + jnp.roll(field, 1, 3)
    return first + second + third


def rates_of(field):
    return diffuse_numbers() * (beside_sum(field) - 6.0 * field)


def react_h(field, feed_rate, kill_rate):
    u = field[0]
    v = field[1]
    uptake = u * v * v
    return jnp.stack([STEP_H * (feed_rate * (1.0 - u) - uptake), STEP_H * (uptake - (feed_rate + kill_rate) * v)])


def relax(right_side, guess):
    diffuse = diffuse_numbers()
    iterate = guess
    for sweep_index in range(SWEEPS):
        iterate = (right_side + diffuse * beside_sum(iterate)) / (1.0 + 6.0 * diffuse)
    return iterate


def reference(state_init, feed_rate, kill_rate):
    weights_table = jnp.asarray(quad_table(STEPS), jnp.float32)
    finals = []
    earlier = None
    for level_index in range(LEVELS):
        history = [state_init]
        current = state_init
        for n in range(STEPS):
            right_side = current + react_h(current, feed_rate, kill_rate)
            if level_index > 0:
                first_node = min(max(n - 1, 0), STEPS - 3)
                source = -react_h(earlier[n], feed_rate, kill_rate) - rates_of(earlier[n + 1])
                for j in range(4):
                    node = earlier[first_node + j]
                    source = source + weights_table[n, j] * (rates_of(node) + react_h(node, feed_rate, kill_rate))
                right_side = right_side + source
            current = relax(right_side, current)
            history.append(current)
        finals.append(current)
        earlier = history
    return jnp.stack(finals)
```

```python
import functools

import jax
import jax.numpy as jnp
import numpy as np
from jax import lax
from jax.experimental import pallas as pl
from jax.experimental.pallas import tpu as pltpu
from jax.sharding import PartitionSpec as P


BRICK = 8
EXT = 3 * BRICK
LANES = 128
AXES = ("level", "gx", "gy")
COEF = (0.5, 0.25)
INV = tuple(1.0 / (1.0 + 6.0 * c) for c in COEF)
MIX = tuple(c / (1.0 + 6.0 * c) for c in COEF)
STEPS = 4
VMEM = pl.BlockSpec(memory_space=pltpu.VMEM)
SMEM = pl.BlockSpec(memory_space=pltpu.SMEM)


def quad_table(step_count):
    table_rows = []
    for n in range(step_count):
        first_node = min(max(n - 1, 0), step_count - 3)
        weights_row = []
        for j in range(4):
            coeffs = [1.0]
            for i in range(4):
                if i != j:
                    shifted = [0.0] + coeffs
                    scaled_terms = [-float(first_node + i) * c for c in coeffs] + [0.0]
                    coeffs = [
                        (shifted[k] + scaled_terms[k]) / float(j - i) for k in range(len(shifted))
                    ]
            integral = 0.0
            for k in range(len(coeffs)):
                integral = integral + coeffs[k] * ((n + 1.0) ** (k + 1) - float(n) ** (k + 1)) / (
                    k + 1.0
                )
            weights_row.append(float(np.float32(integral)))
        table_rows.append(weights_row)
    return table_rows


TABLE = quad_table(STEPS)


def linear(level, gx, gy):
    return (level * 8 + gx) * 8 + gy


def walk(x, level):
    return level if x % 2 == 0 else 3 - level


def device_at(bx, by):
    z, core = bx // 2, bx % 2
    x, place = by // 4, by % 4
    return linear(walk(x, place), (z // 2) * 2 + core, x * 2 + z % 2)


def pairs_along(dim, odd):
    pairs = []
    for bx in range(16):
        for by in range(16):
            at = [bx, by]
            at[dim] = (at[dim] ^ 1) if not odd else (((at[dim] + 1) ^ 1) - 1) % 16
            pairs.append((device_at(bx, by), device_at(*at)))
    return pairs


def spread_pairs():
    pairs = []
    for level in range(4):
        for gx in range(8):
            for gy in range(8):
                x, zl, zh, core = gy // 2, gy % 2, gx // 2, gx % 2
                place = walk(x, level)
                same = place // 2 == zl
                by = 4 * x + (place if same else 3 - place)
                bx = 2 * (2 * zh + core) + (0 if same else 1)
                pairs.append((linear(level, gx, gy), device_at(bx, by)))
    return pairs


def gather_pairs(turn):
    pairs = []
    for bx in range(16):
        for by in range(16):
            piece = 2 * (bx % 2) + by % 2
            pairs.append((device_at(bx, by), linear((piece + turn) % 4, bx // 2, by // 2)))
    return pairs


def swap(array, dim):
    return (
        lax.ppermute(array, AXES, pairs_along(dim, False)),
        lax.ppermute(array, AXES, pairs_along(dim, True)),
    )


def call(kernel, name, out_shapes, args, scratch=()):
    return pl.pallas_call(
        kernel,
        name=name,
        out_shape=[jax.ShapeDtypeStruct(s, jnp.float32) for s in out_shapes],
        in_specs=[SMEM if a.dtype == jnp.int32 else VMEM for a in args],
        out_specs=[VMEM] * len(out_shapes),
        scratch_shapes=[pltpu.VMEM(s, jnp.float32) for s in scratch],
        compiler_params=pltpu.CompilerParams(vmem_limit_bytes=40 << 20),
    )(*args)


def around(prev, cur, nxt):
    second = pltpu.roll(cur, 1, 0) + pltpu.roll(cur, EXT - 1, 0)
    third = pltpu.roll(cur, 1, 1) + pltpu.roll(cur, LANES - 1, 1)
    return (prev + nxt) + (second + third)


def planes(halo):
    return range(BRICK - halo, 2 * BRICK + halo)


def assemble(dst, own, near, far, first):
    for i in range(BRICK):
        for s in range(2):
            dst[s, BRICK + i] = own[first + s, i]
            dst[s, 2 * BRICK + i] = near[first + s, BRICK - 1 - i]
            dst[s, i] = far[first + s, BRICK - 1 - i]


def reacted(u, v, feed, both):
    uptake = u * v * v
    return 0.5 * (feed * (1.0 - u) - uptake), 0.5 * (uptake - both * v)


def advance(dst, field, rates, right, halo, source=None):
    for x in planes(halo - 1):
        u, v = field[0, x], field[1, x]
        du, dv = reacted(u, v, rates[0, x], rates[1, x])
        u, v = u + du, v + dv
        if source is not None:
            u, v = u + source[0, x], v + source[1, x]
        right[0, x] = INV[0] * u
        right[1, x] = INV[1] * v
    src = field
    for k in range(1, 5):
        span = planes(halo - k)
        prev = [src[s, span[0] - 1] for s in range(2)]
        cur = [src[s, span[0]] for s in range(2)]
        for x in span:
            for s in range(2):
                nxt = src[s, x + 1]
                dst[s, x] = right[s, x] + MIX[s] * around(prev[s], cur[s], nxt)
                prev[s], cur[s] = cur[s], nxt
        src = dst


def sources(outs, nodes, first, rates, mixed):
    for n, (out, step, halo) in enumerate(outs):
        linear_w = [TABLE[step][j] - (1.0 if first + j == step + 1 else 0.0) for j in range(4)]
        react_w = [TABLE[step][j] - (1.0 if first + j == step else 0.0) for j in range(4)]
        total = sum(react_w)
        for x in planes(halo + 1):
            us = [node[0, x] for node in nodes]
            vs = [node[1, x] for node in nodes]
            mix_u = sum(w * u for w, u in zip(linear_w, us))
            mix_v = sum(w * v for w, v in zip(linear_w, vs))
            mixed[0, x], mixed[1, x] = mix_u, mix_v
            if x in planes(halo):
                after, now = step + 1 - first, step - first
                sum_u = mix_u + (us[after] - us[now])
                sum_v = mix_v + (vs[after] - vs[now])
                uptake = sum(w * (u * v * v) for w, u, v in zip(react_w, us, vs))
                out[0, x] = 0.5 * (rates[0, x] * (total - sum_u) - uptake)
                out[1, x] = 0.5 * (uptake - rates[1, x] * sum_v)
        span = planes(halo)
        for s in range(2):
            prev, cur = mixed[s, span[0] - 1], mixed[s, span[0]]
            for x in span:
                nxt = mixed[s, x + 1]
                out[s, x] = out[s, x] + COEF[s] * (around(prev, cur, nxt) - 6.0 * cur)
                prev, cur = cur, nxt


def give(dst, first, field):
    for s in range(2):
        for i in range(BRICK):
            dst[first + s, i] = field[s, BRICK + i, BRICK : 2 * BRICK]


def pick_kernel(where, state, feed, kill, out):
    p, q = where[0], where[1]
    rows = pl.ds(pl.multiple_of(q * BRICK, BRICK), BRICK)
    for i in range(BRICK):
        x = jnp.where(p == 0, i, 2 * BRICK - 1 - i)
        out[0, i] = state[0, x, rows]
        out[1, i] = state[1, x, rows]
        out[2, i] = feed[x, rows]
        out[3, i] = kill[x, rows]


def widen_kernel(where, own, near, far, out):
    even = where[2] == 0
    for f in range(own.shape[0]):
        for i in range(BRICK):
            a, b = near[f, i], far[f, i]
            out[f, i, :BRICK] = jnp.where(even, b, a)
            out[f, i, BRICK : 2 * BRICK] = own[f, i]
            out[f, i, 2 * BRICK :] = jnp.where(even, a, b)


def round_0(own, near, far, out, start, rates, y1, y2, right):
    assemble(start, own, near, far, 0)
    assemble(rates, own, near, far, 2)
    for x in range(EXT):
        rates[1, x] = rates[0, x] + rates[1, x]
    advance(y1, start, rates, right, 8)
    advance(y2, y1, rates, right, 4)
    give(out, 0, y2)


def round_1(own, near, far, start, rates, y1, out, y2, y3, y4, z1, s, t, right, mixed):
    assemble(y2, own, near, far, 0)
    advance(y3, y2, rates, right, 8)
    sources([(s, 0, 3), (t, 1, 0)], (start, y1, y2, y3), 0, rates, mixed)
    advance(z1, start, rates, right, 4, s)
    advance(y4, y3, rates, right, 4)
    give(out, 0, z1)
    give(out, 2, t)
    give(out, 4, y4)


def round_2(own, near, far, rates, y1, y2, y3, out, z1, y4, s1, s2, s3, z2, z3, right, mixed):
    assemble(z1, own, near, far, 0)
    assemble(s1, own, near, far, 2)
    assemble(y4, own, near, far, 4)
    advance(z2, z1, rates, right, 8, s1)
    sources([(s2, 2, 3), (s3, 3, 0)], (y1, y2, y3, y4), 1, rates, mixed)
    advance(z3, z2, rates, right, 4, s2)
    give(out, 0, z3)
    give(out, 2, z2)
    give(out, 4, s3)


def round_3(own, near, far, start, rates, y1, out, final, z1, s3, y2, y3, y4, s, z2, right, mixed):
    assemble(y3, own, near, far, 0)
    assemble(y2, own, near, far, 2)
    assemble(s, own, near, far, 4)
    advance(y4, y3, rates, right, 8, s)
    give(final, 0, y4)
    sources([(s, 0, 7), (s3, 1, 3)], (start, y1, y2, y3), 0, rates, mixed)
    advance(z1, start, rates, right, 8, s)
    advance(z2, z1, rates, right, 4, s3)
    sources([(s, 2, 0), (s3, 3, 3)], (y1, y2, y3, y4), 1, rates, mixed)
    give(out, 0, z2)
    give(out, 2, s)


def round_4(own, near, far, start, rates, y1, s3, out, y2, y3, s2, y4, z1, t, right, mixed):
    assemble(y2, own, near, far, 0)
    assemble(s2, own, near, far, 2)
    advance(y3, y2, rates, right, 8, s2)
    sources([(s2, 0, 3), (t, 1, 0)], (start, y1, y2, y3), 0, rates, mixed)
    advance(z1, start, rates, right, 4, s2)
    advance(y4, y3, rates, right, 4, s3)
    give(out, 0, z1)
    give(out, 2, t)
    give(out, 4, y4)


def round_5(own, near, far, rates, y1, y2, y3, out, s3, z1, y4, s1, s2, z2, z3, right, mixed):
    assemble(z1, own, near, far, 0)
    assemble(s1, own, near, far, 2)
    assemble(y4, own, near, far, 4)
    advance(z2, z1, rates, right, 8, s1)
    sources([(s2, 2, 3), (s3, 3, 3)], (y1, y2, y3, y4), 1, rates, mixed)
    advance(z3, z2, rates, right, 4, s2)
    give(out, 0, z3)


def round_6(where, own, near, far, rates, s3, f0, f1, f2, out0, out1, out2, out3, y3, y4, right, last):
    assemble(y3, own, near, far, 0)
    advance(y4, y3, rates, right, 4, s3)
    for i in range(BRICK):
        for s in range(2):
            last[0, s, i] = f0[s, i]
            last[1, s, i] = f1[s, i]
            last[2, s, i] = f2[s, i]
            last[3, s, i] = y4[s, BRICK + i, BRICK : 2 * BRICK]
    turned = where[4]
    for turn, out in enumerate((out0, out1, out2, out3)):
        level = lax.rem(where[3] + turn, 4)
        for i in range(BRICK):
            x = jnp.where(turned == 0, i, BRICK - 1 - i)
            for s in range(2):
                out[s, i] = last[level, s, x]


def place_kernel(where, in0, in1, in2, in3, out):
    for turn, piece in enumerate((in0, in1, in2, in3)):
        at = lax.rem(where[5] + (4 - turn), 4)
        p, q = at // 2, lax.rem(at, 2)
        rows = pl.ds(pl.multiple_of(q * BRICK, BRICK), BRICK)
        for i in range(BRICK):
            for s in range(2):
                out[0, s, p * BRICK + i, rows] = piece[s, i]


def per_device(state, feed, kill):
    level, gx, gy = (lax.axis_index(a) for a in AXES)
    x, low, high, core = gy // 2, gy % 2, gx // 2, gx % 2
    place = jnp.where(x % 2 == 0, level, 3 - level)
    same = place // 2 == low
    where = jnp.stack(
        [
            jnp.where(same, 0, 1),
            jnp.where(same, place, 3 - place) % 2,
            place % 2,
            2 * core + place % 2,
            core,
            level,
        ]
    ).astype(jnp.int32)

    field = (2, EXT, EXT, LANES)

    def send(n):
        return (n, BRICK, BRICK, LANES)

    def exchange(own, name):
        wide = call(
            widen_kernel,
            "widen_" + name,
            [(own.shape[0], BRICK, EXT, LANES)],
            (where, own, *swap(own, 1)),
        )[0]
        return (wide, *swap(wide, 0))

    own = call(pick_kernel, "pick", [send(4)], (where, state, feed, kill))[0]
    own = lax.ppermute(own, AXES, spread_pairs())
    own, start, rates, y1 = call(
        round_0, "round_0", [send(2)] + [field] * 3, exchange(own, "0"), [field] * 2
    )
    own, y2, y3 = call(
        round_1,
        "round_1",
        [send(6), field, field],
        (*exchange(own, "1"), start, rates, y1),
        [field] * 6,
    )
    final_0 = own[4:6]
    own, z1 = call(
        round_2,
        "round_2",
        [send(6), field],
        (*exchange(own, "2"), rates, y1, y2, y3),
        [field] * 8,
    )
    own, final_1, y1, s3 = call(
        round_3,
        "round_3",
        [send(4), send(2), field, field],
        (*exchange(own, "3"), start, rates, z1),
        [field] * 7,
    )
    own, y2, y3 = call(
        round_4,
        "round_4",
        [send(6), field, field],
        (*exchange(own, "4"), start, rates, y1, s3),
        [field] * 6,
    )
    final_2 = own[4:6]
    own, s3 = call(
        round_5,
        "round_5",
        [send(2), field],
        (*exchange(own, "5"), rates, y1, y2, y3),
        [field] * 8,
    )
    outs = call(
        round_6,
        "round_6",
        [send(2)] * 4,
        (where, *exchange(own, "6"), rates, s3, final_0, final_1, final_2),
        [field] * 3 + [(4, 2, BRICK, BRICK, LANES)],
    )
    outs = [lax.ppermute(o, AXES, gather_pairs(turn)) for turn, o in enumerate(outs)]
    return call(place_kernel, "place", [(1, 2, 2 * BRICK, 2 * BRICK, LANES)], (where, *outs))[0]


def solution(mesh):
    return jax.shard_map(
        per_device,
        mesh=mesh,
        in_specs=(P(None, "gx", "gy", None), P("gx", "gy", None), P("gx", "gy", None)),
        out_specs=P("level", None, "gx", "gy", None),
        check_vma=False,
    )
```

```python
import functools

import jax
import jax.numpy as jnp
import numpy as np
from jax import lax
from jax.experimental import pallas as pl
from jax.experimental.pallas import tpu as pltpu
from jax.sharding import PartitionSpec as P


BRICK = 8
EXT = 3 * BRICK
LANES = 128
AXES = ("level", "gx", "gy")
COEF = (0.5, 0.25)
INV = tuple(1.0 / (1.0 + 6.0 * c) for c in COEF)
MIX = tuple(c / (1.0 + 6.0 * c) for c in COEF)
STEPS = 4
VMEM = pl.BlockSpec(memory_space=pltpu.VMEM)
ANY = pl.BlockSpec(memory_space=pl.ANY)


def quad_table(step_count):
    table_rows = []
    for n in range(step_count):
        first_node = min(max(n - 1, 0), step_count - 3)
        weights_row = []
        for j in range(4):
            coeffs = [1.0]
            for i in range(4):
                if i != j:
                    shifted = [0.0] + coeffs
                    scaled_terms = [-float(first_node + i) * c for c in coeffs] + [0.0]
                    coeffs = [
                        (shifted[k] + scaled_terms[k]) / float(j - i) for k in range(len(shifted))
                    ]
            integral = 0.0
            for k in range(len(coeffs)):
                integral = integral + coeffs[k] * ((n + 1.0) ** (k + 1) - float(n) ** (k + 1)) / (
                    k + 1.0
                )
            weights_row.append(float(np.float32(integral)))
        table_rows.append(weights_row)
    return table_rows


TABLE = quad_table(STEPS)


def linear(level, gx, gy):
    return (level * 8 + gx) * 8 + gy


def walk(x, level):
    return level if x % 2 == 0 else 3 - level


def device_at(bx, by):
    z, core = bx // 2, bx % 2
    x, place = by // 4, by % 4
    return linear(walk(x, place), (z // 2) * 2 + core, x * 2 + z % 2)


def pairs_along(dim, odd):
    pairs = []
    for bx in range(16):
        for by in range(16):
            at = [bx, by]
            at[dim] = (at[dim] ^ 1) if not odd else (((at[dim] + 1) ^ 1) - 1) % 16
            pairs.append((device_at(bx, by), device_at(*at)))
    return pairs


def spread_pairs(beside):
    pairs = []
    for level in range(4):
        for gx in range(8):
            for gy in range(8):
                x, zl = gy // 2, gy % 2
                place = walk(x, level)
                same = place // 2 == zl
                by = 4 * x + (place if same else 3 - place)
                if beside:
                    by = (((by + 1) ^ 1) - 1) % 16
                pairs.append((linear(level, gx, gy), device_at(2 * gx + (0 if same else 1), by)))
    return pairs


def gather_pairs(turn):
    pairs = []
    for bx in range(16):
        for by in range(16):
            level = 2 * (bx % 2) + (turn ^ (by % 2))
            pairs.append((device_at(bx, by), linear(level, bx // 2, by // 2)))
    return pairs


def sent(array, dim, odd):
    return lax.ppermute(array, AXES, pairs_along(dim, odd))


def call(kernel, name, out_shapes, args, scratch=(), space=VMEM, out_space=VMEM):
    return pl.pallas_call(
        kernel,
        name=name,
        out_shape=[jax.ShapeDtypeStruct(s, jnp.float32) for s in out_shapes],
        in_specs=[space] * len(args),
        out_specs=[out_space] * len(out_shapes),
        scratch_shapes=[s if not isinstance(s, tuple) else pltpu.VMEM(s, jnp.float32) for s in scratch],
        compiler_params=pltpu.CompilerParams(vmem_limit_bytes=40 << 20),
    )(*args)


def planes(halo):
    return range(BRICK - halo, 2 * BRICK + halo)


OWN = slice(BRICK, 2 * BRICK)


def rows(x, halo):
    away = max(BRICK - x, x - (2 * BRICK - 1), 0)
    return slice(0, EXT) if away < halo else OWN


def around(prev, cur, nxt, at):
    second = pltpu.roll(cur, 1, 0) + pltpu.roll(cur, EXT - 1, 0)
    third = pltpu.roll(cur[at], 1, 1) + pltpu.roll(cur[at], LANES - 1, 1)
    return (prev[at] + nxt[at]) + (second[at] + third)


def reacted(u, v, feed, both):
    uptake = u * v * v
    return 0.5 * (feed * (1.0 - u) - uptake), 0.5 * (uptake - both * v)


def advance(dst, field, rates, right, halo, source=None):
    for x in planes(halo - 1):
        at = rows(x, halo - 1)
        u, v = field[0, x, at], field[1, x, at]
        du, dv = reacted(u, v, rates[0, x, at], rates[1, x, at])
        u, v = u + du, v + dv
        if source is not None:
            u, v = u + source[0, x, at], v + source[1, x, at]
        right[0, x, at] = INV[0] * u
        right[1, x, at] = INV[1] * v
    src = field
    for k in range(1, 5):
        span = planes(halo - k)
        prev = [src[s, span[0] - 1] for s in range(2)]
        cur = [src[s, span[0]] for s in range(2)]
        for x in span:
            at = rows(x, halo - k)
            for s in range(2):
                nxt = src[s, x + 1]
                dst[s, x, at] = right[s, x, at] + MIX[s] * around(prev[s], cur[s], nxt, at)
                prev[s], cur[s] = cur[s], nxt
        src = dst


def sources(outs, nodes, first, rates, mixed):
    for out, step, halo in outs:
        linear_w = [TABLE[step][j] - (1.0 if first + j == step + 1 else 0.0) for j in range(4)]
        react_w = [TABLE[step][j] - (1.0 if first + j == step else 0.0) for j in range(4)]
        total = sum(react_w)
        for x in planes(halo + 1):
            at = rows(x, halo + 1)
            us = [node[0, x, at] for node in nodes]
            vs = [node[1, x, at] for node in nodes]
            mix_u = sum(w * u for w, u in zip(linear_w, us))
            mix_v = sum(w * v for w, v in zip(linear_w, vs))
            mixed[0, x, at], mixed[1, x, at] = mix_u, mix_v
            if x in planes(halo):
                after, now = step + 1 - first, step - first
                sum_u = mix_u + (us[after] - us[now])
                sum_v = mix_v + (vs[after] - vs[now])
                uptake = sum(w * (u * v * v) for w, u, v in zip(react_w, us, vs))
                out[0, x, at] = 0.5 * (rates[0, x, at] * (total - sum_u) - uptake)
                out[1, x, at] = 0.5 * (uptake - rates[1, x, at] * sum_v)
        span = planes(halo)
        for s in range(2):
            prev, cur = mixed[s, span[0] - 1], mixed[s, span[0]]
            for x in span:
                at = rows(x, halo)
                nxt = mixed[s, x + 1]
                out[s, x, at] = out[s, x, at] + COEF[s] * (around(prev, cur, nxt, at) - 6.0 * cur[at])
                prev, cur = cur, nxt


FULL = (1, 8, 7, None, None)
NEAR = (1, 4, 3, 4, 0)
RING_Y = (5, 8, 7, 0, 4)
RING_S = (4, 7, 7, 1, 3)


def tiles_y(kinds):
    return sum(2 if kind is FULL else 1 for kind in kinds)


def tiles_x(kind):
    return kind[1] - kind[0] + 1 + kind[2]


def row_index():
    return lax.broadcasted_iota(jnp.int32, (BRICK, LANES), 0)


def four(first):
    index = row_index()
    return (index >= first) & (index < first + 4)


def even_y():
    return (lax.axis_index("level") + lax.axis_index("gy") // 2) % 2 == 0


def pack_y(outs, kinds, fields):
    even = even_y()
    at = 0
    for kind, field in zip(kinds, fields):
        if kind is not FULL:
            masks = [
                four(jnp.where(even, kind[3], kind[4])),
                four(jnp.where(even, kind[4], kind[3])),
            ]
        for i in range(BRICK):
            u, v = field[0, BRICK + i, OWN], field[1, BRICK + i, OWN]
            if kind is FULL:
                for out in outs:
                    out[at, i], out[at + 1, i] = u, v
            else:
                v = pltpu.roll(v, 4, 0)
                for out, mask in zip(outs, masks):
                    out[at, i] = jnp.where(mask, u, v)
        at += tiles_y([kind])


def widen(kinds, near, far, *refs):
    fields, (wide, to_near, to_far) = refs[: len(kinds)], refs[len(kinds) :]
    even = even_y()
    at = 0
    for f, (kind, field) in enumerate(zip(kinds, fields)):
        for i in range(BRICK):
            for s in range(2):
                tile = at + (s if kind is FULL else 0)
                a, b = near[tile, i], far[tile, i]
                low, high = jnp.where(even, b, a), jnp.where(even, a, b)
                if kind is not FULL and s == 1:
                    low, high = pltpu.roll(low, 4, 0), pltpu.roll(high, 4, 0)
                if kind in (RING_Y, RING_S):
                    low = jnp.where(four(kind[3]), low, field[s, BRICK + i, :BRICK])
                    high = jnp.where(four(kind[4]), high, field[s, BRICK + i, 2 * BRICK :])
                wide[2 * f + s, i, :BRICK] = low
                wide[2 * f + s, i, OWN] = field[s, BRICK + i, OWN]
                wide[2 * f + s, i, 2 * BRICK :] = high
        at += tiles_y([kind])
    pack_x(kinds, wide, to_near, to_far)


def pack_x(kinds, wide, to_near, to_far):
    index = row_index()
    at = 0
    for f, kind in enumerate(kinds):
        first, last, corners = kind[:3]
        for s in range(2):
            field = wide.at[2 * f + s]
            for out, plane in ((to_near, lambda e: BRICK - e), (to_far, lambda e: e - 1)):
                for e in range(first, last + 1):
                    out[at + e - first] = field[plane(e), OWN]
                for e in range(1, corners + 1):
                    low, other = (e, BRICK - e) if corners == 7 else (4, e)
                    out[at + last - first + e] = jnp.where(
                        index >= low, field[plane(e), :BRICK], field[plane(other), 2 * BRICK :]
                    )
            at += tiles_x(kind)


def assemble(kinds, dsts, wide, near, far, bases=()):
    bases = list(bases)
    at = 0
    for f, (kind, dst) in enumerate(zip(kinds, dsts)):
        first, last, corners = kind[:3]
        base = bases.pop(0) if kind in (RING_Y, RING_S) else None
        for s in range(2):
            for i in range(BRICK):
                dst[s, BRICK + i] = wide[2 * f + s, i]
            for ref, plane in ((near, lambda e: 2 * BRICK - 1 + e), (far, lambda e: BRICK - e)):
                for e in range(1, first):
                    dst[s, plane(e), OWN] = base[s, plane(e), OWN]
                for e in range(first, last + 1):
                    dst[s, plane(e), OWN] = ref[at + e - first]
                for e in range(1, corners + 1):
                    other = BRICK - e if corners == 7 else e
                    both = ref[at + last - first + e]
                    dst[s, plane(e), :BRICK] = both
                    dst[s, plane(other), 2 * BRICK :] = both
            at += tiles_x(kind)


def pick(state, feed, kill, pair, brick, state_v, feed_v, kill_v, sems):
    x, low, level = lax.axis_index("gy") // 2, lax.axis_index("gy") % 2, lax.axis_index("level")
    place = jnp.where(x % 2 == 0, level, 3 - level)
    same = place // 2 == low
    q = jnp.where(same, place, 3 - place) % 2
    half = pl.ds(jnp.where(same, 0, BRICK), BRICK)
    copies = [
        pltpu.make_async_copy(state.at[:, half], state_v, sems.at[0]),
        pltpu.make_async_copy(feed.at[half], feed_v, sems.at[1]),
        pltpu.make_async_copy(kill.at[half], kill_v, sems.at[2]),
    ]
    for copy in copies:
        copy.start()
    for copy in copies:
        copy.wait()
    for i in range(BRICK):
        at = jnp.where(same, i, BRICK - 1 - i)
        for f, cells in enumerate((state_v[0, at], state_v[1, at], feed_v[at], kill_v[at])):
            pair[f, i] = cells
            brick[f, i] = jnp.where(q == 0, cells[:BRICK], cells[BRICK:])


def widen_0(pair, far, wide, to_near, to_far):
    even = even_y()
    for f in range(4):
        for i in range(BRICK):
            one, two, three = pair[f, i, :BRICK], pair[f, i, BRICK:], far[f, i]
            wide[f, i, :BRICK] = jnp.where(even, three, one)
            wide[f, i, OWN] = jnp.where(even, one, two)
            wide[f, i, 2 * BRICK :] = jnp.where(even, two, three)
    pack_x((FULL, FULL), wide, to_near, to_far)


KINDS = {
    0: (FULL, FULL),
    1: (FULL,),
    2: (FULL, RING_S, NEAR),
    3: (FULL, RING_Y, RING_S),
    4: (FULL, RING_S),
    5: (FULL, RING_S, NEAR),
    6: (NEAR,),
}


def round_0(wide, near, far, out, start, rates, y1, y2, right):
    assemble(KINDS[0], (start, rates), wide, near, far)
    for x in range(EXT):
        rates[1, x] = rates[0, x] + rates[1, x]
    advance(y1, start, rates, right, 8)
    advance(y2, y1, rates, right, 4)
    pack_y((out,), KINDS[1], (y2,))


def round_1(wide, near, far, start, rates, y1, out_a, out_b, y2, y3, z1, t, y4, s, right, mixed):
    assemble(KINDS[1], (y2,), wide, near, far)
    advance(y3, y2, rates, right, 8)
    sources([(s, 0, 3), (t, 1, 3)], (start, y1, y2, y3), 0, rates, mixed)
    advance(z1, start, rates, right, 4, s)
    advance(y4, y3, rates, right, 4)
    pack_y((out_a, out_b), KINDS[2], (z1, t, y4))


def round_2(wide, near, far, base, rates, y1, y2, y3, out_a, out_b, z1, z3, z2, s3, s1, y4, s2, right, mixed):
    assemble(KINDS[2], (z1, s1, y4), wide, near, far, (base,))
    advance(z2, z1, rates, right, 8, s1)
    sources([(s2, 2, 3), (s3, 3, 3)], (y1, y2, y3, y4), 1, rates, mixed)
    advance(z3, z2, rates, right, 4, s2)
    pack_y((out_a, out_b), KINDS[3], (z3, z2, s3))


def round_3(
    wide, near, far, base_y, base_s, start, rates, y1, out_a, out_b, y4, z1, z2, s2, s3, y2, y3, s, right, mixed
):
    assemble(KINDS[3], (y3, y2, s), wide, near, far, (base_y, base_s))
    advance(y4, y3, rates, right, 8, s)
    sources([(s, 0, 7), (s3, 1, 3)], (start, y1, y2, y3), 0, rates, mixed)
    advance(z1, start, rates, right, 8, s)
    advance(z2, z1, rates, right, 4, s3)
    sources([(s2, 2, 3), (s3, 3, 3)], (y1, y2, y3, y4), 1, rates, mixed)
    pack_y((out_a, out_b), KINDS[4], (z2, s2))


def round_4(
    wide, near, far, base, start, rates, y1, s3, out_a, out_b, y2, y3, z1, t, y4, s2, right, mixed
):
    assemble(KINDS[4], (y2, s2), wide, near, far, (base,))
    advance(y3, y2, rates, right, 8, s2)
    sources([(s2, 0, 3), (t, 1, 3)], (start, y1, y2, y3), 0, rates, mixed)
    advance(z1, start, rates, right, 4, s2)
    advance(y4, y3, rates, right, 4, s3)
    pack_y((out_a, out_b), KINDS[5], (z1, t, y4))


def round_5(wide, near, far, base, rates, y1, y2, y3, out_a, out_b, z3, s3, z1, s1, y4, z2, s2, right, mixed):
    assemble(KINDS[5], (z1, s1, y4), wide, near, far, (base,))
    advance(z2, z1, rates, right, 8, s1)
    sources([(s2, 2, 3), (s3, 3, 3)], (y1, y2, y3, y4), 1, rates, mixed)
    advance(z3, z2, rates, right, 4, s2)
    pack_y((out_a, out_b), KINDS[6], (z3,))


def round_6(wide, near, far, rates, s3, f0, f1, f2, keep, give, y3, y4, right, last):
    assemble(KINDS[6], (y3,), wide, near, far)
    advance(y4, y3, rates, right, 4, s3)
    core = lax.axis_index("gx") % 2
    for i in range(BRICK):
        x = jnp.where(core == 0, i, BRICK - 1 - i)
        for s in range(2):
            for level, field in enumerate((f0, f1, f2, y4)):
                last[level, s, x] = field[s, BRICK + i, OWN]
    for j in range(2):
        keep[j] = last[2 * core + j]
        give[j] = last[2 * (1 - core) + j]


def join(keep, got, out_0, out_1):
    core, odd = lax.axis_index("gx") % 2, jnp.where(even_y(), 0, 1)
    for turn, out in enumerate((out_0, out_1)):
        j = jnp.where(odd == turn, 0, 1)
        for i in range(BRICK):
            for s in range(2):
                out[s, core * BRICK + i] = keep[j, s, i]
                out[s, (1 - core) * BRICK + i] = got[j, s, i]


def put(in_0, in_1, out, sems):
    odd = lax.axis_index("level") % 2
    copies = []
    for turn, piece in enumerate((in_0, in_1)):
        q = jnp.where(odd == turn, 0, 1)
        at = pl.ds(pl.multiple_of(q * BRICK, BRICK), BRICK)
        copies.append(pltpu.make_async_copy(piece, out.at[0, :, :, at], sems.at[turn]))
    for copy in copies:
        copy.start()
    for copy in copies:
        copy.wait()


def per_device(state, feed, kill):
    field = (2, EXT, EXT, LANES)
    block = (2, 2 * BRICK, 2 * BRICK, LANES)

    def brick(n):
        return (n, BRICK, BRICK, LANES)

    def sends(n):
        return [brick(tiles_y(KINDS[n]))] * 2

    def wide_shapes(n):
        count = len(KINDS[n])
        flat = (2 * sum(tiles_x(kind) for kind in KINDS[n]), BRICK, LANES)
        return [(2 * count, BRICK, EXT, LANES), flat, flat]

    def along_x(wide, to_near, to_far):
        return wide, sent(to_near, 0, False), sent(to_far, 0, True)

    def exchange(n, to_near, to_far, *fields):
        got = sent(to_near, 1, False), sent(to_far, 1, True)
        kernel = functools.partial(widen, KINDS[n])
        return along_x(*call(kernel, f"widen_{n}", wide_shapes(n), (*got, *fields)))

    half = (BRICK, 2 * BRICK, LANES)
    pair, one = call(
        pick,
        "pick",
        [(4,) + half, brick(4)],
        (state, feed, kill),
        [(2,) + half, half, half, pltpu.SemaphoreType.DMA((3,))],
        space=ANY,
    )
    pair = lax.ppermute(pair, AXES, spread_pairs(False))
    one = lax.ppermute(one, AXES, spread_pairs(True))
    wide = along_x(*call(widen_0, "widen_0", wide_shapes(0), (pair, one)))
    out, start, rates, y1, y2 = call(
        round_0, "round_0", [brick(2)] + [field] * 4, wide, [field]
    )
    wide = exchange(1, out, out, y2)
    *out, y2, y3, z1, t, final_0 = call(
        round_1, "round_1", sends(2) + [field] * 5, (*wide, start, rates, y1), [field] * 3
    )
    wide = exchange(2, *out, z1, t, final_0)
    *out, z1, z3, z2, s3 = call(
        round_2, "round_2", sends(3) + [field] * 4, (*wide, t, rates, y1, y2, y3), [field] * 5
    )
    wide = exchange(3, *out, z3, z2, s3)
    *out, final_1, y1, y2, s2, s4 = call(
        round_3, "round_3", sends(4) + [field] * 5, (*wide, z2, s3, start, rates, z1), [field] * 5
    )
    wide = exchange(4, *out, y2, s2)
    *out, y2, y3, z1, t, final_2 = call(
        round_4, "round_4", sends(5) + [field] * 5, (*wide, s2, start, rates, y1, s4), [field] * 3
    )
    wide = exchange(5, *out, z1, t, final_2)
    *out, z3, s3 = call(
        round_5, "round_5", sends(6) + [field] * 2, (*wide, t, rates, y1, y2, y3), [field] * 7
    )
    wide = exchange(6, *out, z3)
    keep, give = call(
        round_6,
        "round_6",
        [(2,) + brick(2)] * 2,
        (*wide, rates, s3, final_0, final_1, final_2),
        [field] * 3 + [(4,) + brick(2)],
    )
    half = (2, 2 * BRICK, BRICK, LANES)
    outs = call(join, "join", [half] * 2, (keep, sent(give, 0, False)))
    outs = [lax.ppermute(o, AXES, gather_pairs(turn)) for turn, o in enumerate(outs)]
    return call(
        put, "put", [(1,) + block], outs, [pltpu.SemaphoreType.DMA((2,))], out_space=ANY
    )[0]


def solution(mesh):
    return jax.shard_map(
        per_device,
        mesh=mesh,
        in_specs=(P(None, "gx", "gy", None), P("gx", "gy", None), P("gx", "gy", None)),
        out_specs=P("level", None, "gx", "gy", None),
        check_vma=False,
    )
```

```python
import functools
import itertools

import jax
import jax.numpy as jnp
import numpy as np
from jax import lax
from jax.experimental import pallas as pl
from jax.experimental.pallas import tpu as pltpu
from jax.sharding import PartitionSpec as P


BRICK = 8
EXT = 3 * BRICK
LANES = 128
AXES = ("level", "gx", "gy")
COEF = (0.5, 0.25)
INV = tuple(1.0 / (1.0 + 6.0 * c) for c in COEF)
MIX = tuple(c / (1.0 + 6.0 * c) for c in COEF)
STEPS = 4
VMEM = pl.BlockSpec(memory_space=pltpu.VMEM)
HBM = pl.BlockSpec(memory_space=pltpu.HBM)


def quad_table(step_count):
    table_rows = []
    for n in range(step_count):
        first_node = min(max(n - 1, 0), step_count - 3)
        weights_row = []
        for j in range(4):
            coeffs = [1.0]
            for i in range(4):
                if i != j:
                    shifted = [0.0] + coeffs
                    scaled_terms = [-float(first_node + i) * c for c in coeffs] + [0.0]
                    coeffs = [
                        (shifted[k] + scaled_terms[k]) / float(j - i) for k in range(len(shifted))
                    ]
            integral = 0.0
            for k in range(len(coeffs)):
                integral = integral + coeffs[k] * ((n + 1.0) ** (k + 1) - float(n) ** (k + 1)) / (
                    k + 1.0
                )
            weights_row.append(float(np.float32(integral)))
        table_rows.append(weights_row)
    return table_rows


TABLE = quad_table(STEPS)


def linear(level, gx, gy):
    return (level * 8 + gx) * 8 + gy


WALK = (
    *((0, 0), (0, 1), (0, 2), (0, 3)),
    *((1, 3), (1, 2), (1, 1), (1, 0)),
    *((2, 0), (2, 1), (2, 2), (2, 3)),
    *((3, 3), (3, 2), (3, 1), (3, 0)),
)


def device_at(bx, by):
    (x, y), z = WALK[by], bx // 2
    core = (bx + (z % 4 != 3)) % 2
    return linear(y, (z // 2) * 2 + core, x * 2 + z % 2)


def odd_x():
    z = (lax.axis_index("gx") // 2) * 2 + lax.axis_index("gy") % 2
    return (lax.axis_index("gx") + jnp.where(z % 4 != 3, 1, 0)) % 2


def assigned(gy):
    def cost(pieces):
        return sum(abs(level - WALK[2 * gy + q][1]) for level, (p, q) in enumerate(pieces))

    return min(itertools.permutations(itertools.product(range(2), repeat=2)), key=cost)


def pairs_along(dim, odd):
    pairs = []
    for bx in range(16):
        for by in range(16):
            at = [bx, by]
            at[dim] = (at[dim] ^ 1) if not odd else (((at[dim] + 1) ^ 1) - 1) % 16
            pairs.append((device_at(bx, by), device_at(*at)))
    return pairs


def spread_pairs(beside):
    pairs = []
    for level in range(4):
        for gx in range(8):
            for gy in range(8):
                p, q = assigned(gy)[level]
                by = 2 * gy + q
                if beside:
                    by = (((by + 1) ^ 1) - 1) % 16
                pairs.append((linear(level, gx, gy), device_at(2 * gx + p, by)))
    return pairs


def gather_pairs(turn):
    pairs = []
    for bx in range(16):
        for by in range(16):
            level = 2 * (bx % 2) + (turn ^ (by % 2))
            pairs.append((device_at(bx, by), linear(level, bx // 2, by // 2)))
    return pairs


def sent(array, dim, odd):
    return lax.ppermute(array, AXES, pairs_along(dim, odd))


def call(kernel, name, out_shapes, args, scratch=(), space=VMEM, out_space=VMEM, limit=40):
    return pl.pallas_call(
        kernel,
        name=name,
        out_shape=[jax.ShapeDtypeStruct(s, jnp.float32) for s in out_shapes],
        in_specs=[space] * len(args),
        out_specs=[out_space] * len(out_shapes),
        scratch_shapes=[s if not isinstance(s, tuple) else pltpu.VMEM(s, jnp.float32) for s in scratch],
        compiler_params=pltpu.CompilerParams(vmem_limit_bytes=limit << 20),
    )(*args)


def planes(halo):
    return range(BRICK - halo, 2 * BRICK + halo)


OWN = slice(BRICK, 2 * BRICK)


def rows(x, halo):
    away = max(BRICK - x, x - (2 * BRICK - 1), 0)
    return slice(0, EXT) if away < halo else OWN


def around(prev, cur, nxt, at):
    count = cur.shape[0]
    second = pltpu.roll(cur, 1, 0) + pltpu.roll(cur, count - 1, 0)
    third = pltpu.roll(cur[at], 1, 1) + pltpu.roll(cur[at], LANES - 1, 1)
    return (prev[at] + nxt[at]) + (second[at] + third)


FIRST, SLIM = slice(0, BRICK), slice(0, 2 * BRICK)


def slim(ref, s, x):
    cells = ref[s, x]
    halo = jnp.where(row_index() < 4, cells[2 * BRICK :], cells[:BRICK])
    return jnp.concatenate([cells[OWN], halo], axis=0)


def row_index():
    return lax.broadcasted_iota(jnp.int32, (BRICK, LANES), 0)


def reacted(u, v, feed, both):
    uptake = u * v * v
    return 0.5 * (feed * (1.0 - u) - uptake), 0.5 * (uptake - both * v)


def whole(ref, s, x):
    return ref[s, x]


def advance(dst, field, rates, right, halo, source=None):
    thin = halo == 4
    load, own, full = (slim, FIRST, SLIM) if thin else (whole, OWN, slice(0, EXT))

    def part(x, halo):
        return own if rows(x, halo) == OWN else full

    for x in planes(halo - 1):
        at = part(x, halo - 1)
        u, v = load(field, 0, x)[at], load(field, 1, x)[at]
        du, dv = reacted(u, v, load(rates, 0, x)[at], load(rates, 1, x)[at])
        u, v = u + du, v + dv
        if source is not None:
            u, v = u + load(source, 0, x)[at], v + load(source, 1, x)[at]
        right[0, x, at] = INV[0] * u
        right[1, x, at] = INV[1] * v
    for k in range(1, 5):

        def get(s, x):
            return load(field, s, x) if k == 1 else dst[s, x, full]

        span = planes(halo - k)
        prev = [get(s, span[0] - 1) for s in range(2)]
        cur = [get(s, span[0]) for s in range(2)]
        for x in span:
            at = part(x, halo - k)
            for s in range(2):
                nxt = get(s, x + 1)
                new = right[s, x, at] + MIX[s] * around(prev[s], cur[s], nxt, at)
                dst[s, x, OWN if k == halo else at] = new
                prev[s], cur[s] = cur[s], nxt


def sources(outs, nodes, first, rates, mixed):
    for out, step, halo in outs:
        thin = halo == 3
        load, own, full = (slim, FIRST, SLIM) if thin else (whole, OWN, slice(0, EXT))
        linear_w = [TABLE[step][j] - (1.0 if first + j == step + 1 else 0.0) for j in range(4)]
        react_w = [TABLE[step][j] - (1.0 if first + j == step else 0.0) for j in range(4)]
        total = sum(react_w)
        for x in planes(halo + 1):
            at = own if rows(x, halo + 1) == OWN else full
            us = [load(node, 0, x)[at] for node in nodes]
            vs = [load(node, 1, x)[at] for node in nodes]
            mix_u = sum(w * u for w, u in zip(linear_w, us))
            mix_v = sum(w * v for w, v in zip(linear_w, vs))
            mixed[0, x, at], mixed[1, x, at] = mix_u, mix_v
            if x in planes(halo):
                after, now = step + 1 - first, step - first
                sum_u = mix_u + (us[after] - us[now])
                sum_v = mix_v + (vs[after] - vs[now])
                uptake = sum(w * (u * v * v) for w, u, v in zip(react_w, us, vs))
                out[0, x, at] = 0.5 * (load(rates, 0, x)[at] * (total - sum_u) - uptake)
                out[1, x, at] = 0.5 * (uptake - load(rates, 1, x)[at] * sum_v)
        span = planes(halo)
        for s in range(2):
            prev, cur = mixed[s, span[0] - 1, full], mixed[s, span[0], full]
            for x in span:
                at = own if rows(x, halo) == OWN else full
                nxt = mixed[s, x + 1, full]
                new = out[s, x, at] + COEF[s] * (around(prev, cur, nxt, at) - 6.0 * cur[at])
                if thin:
                    out[s, x, OWN] = new[FIRST]
                    if at == full:
                        out[s, x, :BRICK] = out[s, x, 2 * BRICK :] = new[BRICK:]
                else:
                    out[s, x, at] = new
                prev, cur = cur, nxt


FULL = (1, 8, 7, None, None)
NEAR = (1, 4, 3, 4, 0)
RING_Y = (5, 8, 7, 0, 4)
RING_S = (4, 7, 7, 1, 3)


def tiles_y(kinds):
    return sum(2 if kind is FULL else 1 for kind in kinds)


def tiles_x(kind):
    return kind[1] - kind[0] + 1 + kind[2]


def four(first):
    index = row_index()
    return (index >= first) & (index < first + 4)


def even_y():
    return (lax.axis_index("level") + lax.axis_index("gy") // 2) % 2 == 0


def tiles_c(kinds):
    return sum(2 * (kind[1] - kind[0] + 1) for kind in kinds)


def pack_c(out, kinds, fields):
    at = 0
    for kind, field in zip(kinds, fields):
        for s in range(2):
            for e in range(kind[0], kind[1] + 1):
                out[at] = field[s, BRICK + e - 1, OWN]
                at += 1


def pack_y(outs, kinds, fields):
    *outs, centre = outs
    pack_c(centre, kinds, fields)
    even = even_y()
    at = 0
    for kind, field in zip(kinds, fields):
        if kind is not FULL:
            masks = [
                four(jnp.where(even, kind[3], kind[4])),
                four(jnp.where(even, kind[4], kind[3])),
            ]
        for i in range(BRICK):
            u, v = field[0, BRICK + i, OWN], field[1, BRICK + i, OWN]
            if kind is FULL:
                for out in outs:
                    out[at, i], out[at + 1, i] = u, v
            else:
                v = pltpu.roll(v, 4, 0)
                for out, mask in zip(outs, masks):
                    out[at, i] = jnp.where(mask, u, v)
        at += tiles_y([kind])


def widen(kinds, near, far, *refs):
    fields, (_, wide, to_near, to_far) = refs[: len(kinds)], refs[len(kinds) :]
    even = even_y()
    at = 0
    for f, (kind, field) in enumerate(zip(kinds, fields)):
        for i in range(BRICK):
            for s in range(2):
                tile = at + (s if kind is FULL else 0)
                a, b = near[tile, i], far[tile, i]
                low, high = jnp.where(even, b, a), jnp.where(even, a, b)
                if kind is not FULL and s == 1:
                    low, high = pltpu.roll(low, 4, 0), pltpu.roll(high, 4, 0)
                if kind in (RING_Y, RING_S):
                    low = jnp.where(four(kind[3]), low, field[s, BRICK + i, :BRICK])
                    high = jnp.where(four(kind[4]), high, field[s, BRICK + i, 2 * BRICK :])
                wide[2 * f + s, i, :BRICK] = low
                wide[2 * f + s, i, OWN] = field[s, BRICK + i, OWN]
                wide[2 * f + s, i, 2 * BRICK :] = high
        at += tiles_y([kind])
    pack_x(kinds, wide, to_near, to_far, True)


def pack_x(kinds, wide, to_near, to_far, ahead):
    index = row_index()
    at = late = 0
    for f, kind in enumerate(kinds):
        first, last, corners = kind[:3]
        for s in range(2):
            field = wide.at[2 * f + s]
            for out, plane, short in ((to_near, lambda e: BRICK - e, False), (to_far, lambda e: e - 1, ahead)):
                start = late if short else at + last - first + 1
                if not short:
                    for e in range(first, last + 1):
                        out[at + e - first] = field[plane(e), OWN]
                for e in range(1, corners + 1):
                    low, other = (e, BRICK - e) if corners == 7 else (4, e)
                    out[start + e - 1] = jnp.where(
                        index >= low, field[plane(e), :BRICK], field[plane(other), 2 * BRICK :]
                    )
            at += tiles_x(kind)
            late += corners


def assemble(kinds, dsts, wide, near, far, centre=None, bases=()):
    bases = list(bases)
    at = late = ahead = 0
    for f, (kind, dst) in enumerate(zip(kinds, dsts)):
        first, last, corners = kind[:3]
        base = bases.pop(0) if kind in (RING_Y, RING_S) else None
        for s in range(2):
            for i in range(BRICK):
                dst[s, BRICK + i] = wide[2 * f + s, i]
            short = centre is not None
            for ref, own, first_at, start, plane in (
                (near, near, at, at + last - first + 1, lambda e: 2 * BRICK - 1 + e),
                (
                    far,
                    centre if short else far,
                    ahead if short else at,
                    late if short else at + last - first + 1,
                    lambda e: BRICK - e,
                ),
            ):
                for e in range(1, first):
                    dst[s, plane(e), OWN] = base[s, plane(e), OWN]
                for e in range(first, last + 1):
                    dst[s, plane(e), OWN] = own[first_at + e - first]
                for e in range(1, corners + 1):
                    other = BRICK - e if corners == 7 else e
                    both = ref[start + e - 1]
                    dst[s, plane(e), :BRICK] = both
                    dst[s, plane(other), 2 * BRICK :] = both
            at += tiles_x(kind)
            ahead += last - first + 1
            late += corners


def pick(state, feed, kill, pair, brick, state_v, feed_v, kill_v, sems):
    here = lax.axis_index("gy") * 4 + lax.axis_index("level")
    p, q = (
        sum(
            jnp.where(here == gy * 4 + level, 1, 0)
            for gy in range(8)
            for level in range(4)
            if assigned(gy)[level][axis]
        )
        for axis in range(2)
    )
    half = pl.ds(p * BRICK, BRICK)
    copies = [
        pltpu.make_async_copy(state.at[:, half], state_v, sems.at[0]),
        pltpu.make_async_copy(feed.at[half], feed_v, sems.at[1]),
        pltpu.make_async_copy(kill.at[half], kill_v, sems.at[2]),
    ]
    for copy in copies:
        copy.start()
    for copy in copies:
        copy.wait()
    for i in range(BRICK):
        for f, cells in enumerate((state_v[0, i], state_v[1, i], feed_v[i], kill_v[i])):
            pair[f, i] = cells
            brick[f, i] = jnp.where(q == 0, cells[:BRICK], cells[BRICK:])


def widen_0(pair, far, wide, to_near, to_far):
    even = even_y()
    odd = odd_x()
    for f in range(4):
        for i in range(BRICK):
            at = jnp.where(odd == 0, i, BRICK - 1 - i)
            one, two, three = pair[f, at, :BRICK], pair[f, at, BRICK:], far[f, at]
            wide[f, i, :BRICK] = jnp.where(even, three, one)
            wide[f, i, OWN] = jnp.where(even, one, two)
            wide[f, i, 2 * BRICK :] = jnp.where(even, two, three)
    pack_x((FULL, FULL), wide, to_near, to_far, False)


KINDS = {
    0: (FULL, FULL),
    1: (FULL,),
    2: (FULL, RING_S, NEAR),
    3: (FULL, RING_Y, RING_S),
    4: (FULL, RING_S),
    5: (FULL, RING_S, NEAR),
    6: (NEAR,),
}


def round_0(wide, near, far, out, out_c, start, rates, y1, y2, right):
    assemble(KINDS[0], (start, rates), wide, near, far)
    for x in range(EXT):
        rates[1, x] = rates[0, x] + rates[1, x]
    advance(y1, start, rates, right, 8)
    advance(y2, y1, rates, right, 4)
    pack_y((out, out_c), KINDS[1], (y2,))


def round_1(wide, near, far, centre, start, rates, y1, out_a, out_b, out_c, y2, y3, z1, t, y4, s, right, mixed):
    assemble(KINDS[1], (y2,), wide, near, far, centre)
    advance(y3, y2, rates, right, 8)
    sources([(s, 0, 3), (t, 1, 3)], (start, y1, y2, y3), 0, rates, mixed)
    advance(z1, start, rates, right, 4, s)
    advance(y4, y3, rates, right, 4)
    pack_y((out_a, out_b, out_c), KINDS[2], (z1, t, y4))


def round_2(wide, near, far, centre, base, rates, y1, y2, y3, out_a, out_b, out_c, z1, z3, z2, s3, s1, y4, s2, right, mixed):
    assemble(KINDS[2], (z1, s1, y4), wide, near, far, centre, (base,))
    advance(z2, z1, rates, right, 8, s1)
    sources([(s2, 2, 3), (s3, 3, 3)], (y1, y2, y3, y4), 1, rates, mixed)
    advance(z3, z2, rates, right, 4, s2)
    pack_y((out_a, out_b, out_c), KINDS[3], (z3, z2, s3))


def round_3(
    wide, near, far, centre, base_y, base_s, start, rates, y1, out_a, out_b, out_c, y4, z1, z2, s2, s3, y2, y3, s, right, mixed
):
    assemble(KINDS[3], (y3, y2, s), wide, near, far, centre, (base_y, base_s))
    advance(y4, y3, rates, right, 8, s)
    sources([(s, 0, 7), (s3, 1, 3)], (start, y1, y2, y3), 0, rates, mixed)
    advance(z1, start, rates, right, 8, s)
    advance(z2, z1, rates, right, 4, s3)
    sources([(s2, 2, 3), (s3, 3, 3)], (y1, y2, y3, y4), 1, rates, mixed)
    pack_y((out_a, out_b, out_c), KINDS[4], (z2, s2))


def round_4(
    wide, near, far, centre, base, start, rates, y1, s3, out_a, out_b, out_c, y2, y3, z1, t, y4, s2, right, mixed
):
    assemble(KINDS[4], (y2, s2), wide, near, far, centre, (base,))
    advance(y3, y2, rates, right, 8, s2)
    sources([(s2, 0, 3), (t, 1, 3)], (start, y1, y2, y3), 0, rates, mixed)
    advance(z1, start, rates, right, 4, s2)
    advance(y4, y3, rates, right, 4, s3)
    pack_y((out_a, out_b, out_c), KINDS[5], (z1, t, y4))


def round_5(wide, near, far, centre, base, rates, y1, y2, y3, out_a, out_b, out_c, z3, s3, z1, s1, y4, z2, s2, right, mixed):
    assemble(KINDS[5], (z1, s1, y4), wide, near, far, centre, (base,))
    advance(z2, z1, rates, right, 8, s1)
    sources([(s2, 2, 3), (s3, 3, 3)], (y1, y2, y3, y4), 1, rates, mixed)
    advance(z3, z2, rates, right, 4, s2)
    pack_y((out_a, out_b, out_c), KINDS[6], (z3,))


def round_6(wide, near, far, centre, rates, s3, f0, f1, f2, keep, give, y3, y4, right, last):
    assemble(KINDS[6], (y3,), wide, near, far, centre)
    advance(y4, y3, rates, right, 4, s3)
    half = odd_x()
    for i in range(BRICK):
        x = jnp.where(half == 0, i, BRICK - 1 - i)
        for s in range(2):
            for level, field in enumerate((f0, f1, f2, y4)):
                last[level, s, x] = field[s, BRICK + i, OWN]
    for j in range(2):
        keep[j] = last[2 * half + j]
        give[j] = last[2 * (1 - half) + j]


def join(keep, got, out_0, out_1):
    half, odd = odd_x(), jnp.where(even_y(), 0, 1)
    for turn, out in enumerate((out_0, out_1)):
        j = jnp.where(odd == turn, 0, 1)
        for i in range(BRICK):
            for s in range(2):
                out[s, half * BRICK + i] = keep[j, s, i]
                out[s, (1 - half) * BRICK + i] = got[j, s, i]


def put(in_0, in_1, out, sems):
    odd = lax.axis_index("level") % 2
    copies = []
    for turn, piece in enumerate((in_0, in_1)):
        q = jnp.where(odd == turn, 0, 1)
        at = pl.ds(pl.multiple_of(q * BRICK, BRICK), BRICK)
        copies.append(pltpu.make_async_copy(piece, out.at[0, :, :, at], sems.at[turn]))
    for copy in copies:
        copy.start()
    for copy in copies:
        copy.wait()


def per_device(state, feed, kill):
    field = (2, EXT, EXT, LANES)
    block = (2, 2 * BRICK, 2 * BRICK, LANES)

    def brick(n):
        return (n, BRICK, BRICK, LANES)

    def sends(n):
        return [brick(tiles_y(KINDS[n]))] * 2 + [(tiles_c(KINDS[n]), BRICK, LANES)]

    def wide_shapes(n):
        count = len(KINDS[n])
        near = 2 * sum(tiles_x(kind) for kind in KINDS[n])
        far = 2 * sum(kind[2] for kind in KINDS[n]) if n else near
        return [(2 * count, BRICK, EXT, LANES), (near, BRICK, LANES), (far, BRICK, LANES)]

    def along_x(wide, to_near, to_far):
        return wide, sent(to_near, 0, False), sent(to_far, 0, True)

    def exchange(n, to_near, to_far, centre, *fields):
        got = sent(to_near, 1, False), sent(to_far, 1, True)
        centre = sent(centre, 0, True)
        kernel = functools.partial(widen, KINDS[n])
        return (*along_x(*call(kernel, f"widen_{n}", wide_shapes(n), (*got, *fields, centre))), centre)

    part = (BRICK, 2 * BRICK, LANES)
    pair, one = call(
        pick,
        "pick",
        [(4, BRICK, 2 * BRICK, LANES), brick(4)],
        (state, feed, kill),
        [(2,) + part, part, part, pltpu.SemaphoreType.DMA((3,))],
        space=HBM,
        limit=63,
    )
    pair = lax.ppermute(pair, AXES, spread_pairs(False))
    one = lax.ppermute(one, AXES, spread_pairs(True))
    wide = along_x(*call(widen_0, "widen_0", wide_shapes(0), (pair, one)))
    out, centre, start, rates, y1, y2 = call(
        round_0, "round_0", sends(1)[1:] + [field] * 4, wide, [field]
    )
    wide = exchange(1, out, out, centre, y2)
    *out, y2, y3, z1, t, final_0 = call(
        round_1, "round_1", sends(2) + [field] * 5, (*wide, start, rates, y1), [field] * 3
    )
    wide = exchange(2, *out, z1, t, final_0)
    *out, z1, z3, z2, s3 = call(
        round_2, "round_2", sends(3) + [field] * 4, (*wide, t, rates, y1, y2, y3), [field] * 5
    )
    wide = exchange(3, *out, z3, z2, s3)
    *out, final_1, y1, y2, s2, s4 = call(
        round_3, "round_3", sends(4) + [field] * 5, (*wide, z2, s3, start, rates, z1), [field] * 5
    )
    wide = exchange(4, *out, y2, s2)
    *out, y2, y3, z1, t, final_2 = call(
        round_4, "round_4", sends(5) + [field] * 5, (*wide, s2, start, rates, y1, s4), [field] * 3
    )
    wide = exchange(5, *out, z1, t, final_2)
    *out, z3, s3 = call(
        round_5, "round_5", sends(6) + [field] * 2, (*wide, t, rates, y1, y2, y3), [field] * 7
    )
    wide = exchange(6, *out, z3)
    keep, give = call(
        round_6,
        "round_6",
        [(2,) + brick(2)] * 2,
        (*wide, rates, s3, final_0, final_1, final_2),
        [field] * 3 + [(4,) + brick(2)],
    )
    half = (2, 2 * BRICK, BRICK, LANES)
    outs = call(join, "join", [half] * 2, (keep, sent(give, 0, False)))
    outs = [lax.ppermute(o, AXES, gather_pairs(turn)) for turn, o in enumerate(outs)]
    return call(
        put, "put", [(1,) + block], outs, [pltpu.SemaphoreType.DMA((2,))], out_space=HBM
    )[0]


def solution(mesh):
    return jax.shard_map(
        per_device,
        mesh=mesh,
        in_specs=(P(None, "gx", "gy", None), P("gx", "gy", None), P("gx", "gy", None)),
        out_specs=P("level", None, "gx", "gy", None),
        check_vma=False,
    )
```

```python
import functools

import jax
import jax.numpy as jnp
import numpy as np
from jax import lax
from jax.experimental import pallas as pl
from jax.experimental.pallas import tpu as pltpu
from jax.sharding import PartitionSpec as P


BRICK = 8
EXT = 3 * BRICK
LANES = 128
AXES = ("level", "gx", "gy")
COEF = (0.5, 0.25)
INV = tuple(1.0 / (1.0 + 6.0 * c) for c in COEF)
MIX = tuple(c / (1.0 + 6.0 * c) for c in COEF)
STEPS = 4
VMEM = pl.BlockSpec(memory_space=pltpu.VMEM)
HBM = pl.BlockSpec(memory_space=pltpu.HBM)


def quad_table(step_count):
    table_rows = []
    for n in range(step_count):
        first_node = min(max(n - 1, 0), step_count - 3)
        weights_row = []
        for j in range(4):
            coeffs = [1.0]
            for i in range(4):
                if i != j:
                    shifted = [0.0] + coeffs
                    scaled_terms = [-float(first_node + i) * c for c in coeffs] + [0.0]
                    coeffs = [
                        (shifted[k] + scaled_terms[k]) / float(j - i) for k in range(len(shifted))
                    ]
            integral = 0.0
            for k in range(len(coeffs)):
                integral = integral + coeffs[k] * ((n + 1.0) ** (k + 1) - float(n) ** (k + 1)) / (
                    k + 1.0
                )
            weights_row.append(float(np.float32(integral)))
        table_rows.append(weights_row)
    return table_rows


TABLE = quad_table(STEPS)


def linear(level, gx, gy):
    return (level * 8 + gx) * 8 + gy


WALK = (
    *((0, 0), (0, 1), (0, 2), (0, 3)),
    *((1, 3), (1, 2), (1, 1), (1, 0)),
    *((2, 0), (2, 1), (2, 2), (2, 3)),
    *((3, 3), (3, 2), (3, 1), (3, 0)),
)


def device_at(bx, by):
    (x, y), z = WALK[by], bx // 2
    core = (bx + (z % 4 != 3)) % 2
    return linear(y, (z // 2) * 2 + core, x * 2 + z % 2)


def odd_x():
    z = (lax.axis_index("gx") // 2) * 2 + lax.axis_index("gy") % 2
    return (lax.axis_index("gx") + jnp.where(z % 4 != 3, 1, 0)) % 2


def pairs_along(dim, odd):
    pairs = []
    for bx in range(16):
        for by in range(16):
            at = [bx, by]
            at[dim] = (at[dim] ^ 1) if not odd else (((at[dim] + 1) ^ 1) - 1) % 16
            pairs.append((device_at(bx, by), device_at(*at)))
    return pairs


def first_sent(level, x):
    return level // 2, level % 2, (level // 2 + x) % 2


def spread_pairs(beside):
    pairs = []
    for level in range(4):
        for gx in range(8):
            for gy in range(8):
                p, far_p, far_q = first_sent(level, gy // 2)
                bx, by = 2 * gx + p, 2 * gy + ((level + 1) // 2 + gy) % 2
                if beside:
                    bx, by = 2 * gx + far_p, (((2 * gy + far_q + 1) ^ 1) - 1) % 16
                pairs.append((linear(level, gx, gy), device_at(bx, by)))
    return pairs


def gather_pairs(turn):
    pairs = []
    for bx in range(16):
        for by in range(16):
            level = 2 * (bx % 2) + (turn ^ (by % 2))
            pairs.append((device_at(bx, by), linear(level, bx // 2, by // 2)))
    return pairs


def sent(array, dim, odd):
    return lax.ppermute(array, AXES, pairs_along(dim, odd))


def call(kernel, name, out_shapes, args, scratch=(), space=VMEM, out_space=VMEM, limit=40):
    return pl.pallas_call(
        kernel,
        name=name,
        out_shape=[jax.ShapeDtypeStruct(s, jnp.float32) for s in out_shapes],
        in_specs=[space] * len(args),
        out_specs=[out_space] * len(out_shapes),
        scratch_shapes=[s if not isinstance(s, tuple) else pltpu.VMEM(s, jnp.float32) for s in scratch],
        compiler_params=pltpu.CompilerParams(vmem_limit_bytes=limit << 20),
    )(*args)


def planes(halo):
    return range(BRICK - halo, 2 * BRICK + halo)


OWN = slice(BRICK, 2 * BRICK)


def rows(x, halo):
    away = max(BRICK - x, x - (2 * BRICK - 1), 0)
    return slice(0, EXT) if away < halo else OWN


def around(prev, cur, nxt, at):
    count = cur.shape[0]
    second = pltpu.roll(cur, 1, 0) + pltpu.roll(cur, count - 1, 0)
    third = pltpu.roll(cur[at], 1, 1) + pltpu.roll(cur[at], LANES - 1, 1)
    return (prev[at] + nxt[at]) + (second[at] + third)


FIRST, SLIM = slice(0, BRICK), slice(0, 2 * BRICK)


def slim(ref, s, x):
    cells = ref[s, x]
    halo = jnp.where(row_index() < 4, cells[2 * BRICK :], cells[:BRICK])
    return jnp.concatenate([cells[OWN], halo], axis=0)


def row_index():
    return lax.broadcasted_iota(jnp.int32, (BRICK, LANES), 0)


def reacted(u, v, feed, both):
    uptake = u * v * v
    return 0.5 * (feed * (1.0 - u) - uptake), 0.5 * (uptake - both * v)


def whole(ref, s, x):
    return ref[s, x]


def advance(dst, field, rates, right, halo, source=None):
    thin = halo == 4
    load, own, full = (slim, FIRST, SLIM) if thin else (whole, OWN, slice(0, EXT))

    def part(x, halo):
        return own if rows(x, halo) == OWN else full

    for x in planes(halo - 1):
        at = part(x, halo - 1)
        u, v = load(field, 0, x)[at], load(field, 1, x)[at]
        du, dv = reacted(u, v, load(rates, 0, x)[at], load(rates, 1, x)[at])
        u, v = u + du, v + dv
        if source is not None:
            u, v = u + load(source, 0, x)[at], v + load(source, 1, x)[at]
        right[0, x, at] = INV[0] * u
        right[1, x, at] = INV[1] * v
    for k in range(1, 5):

        def get(s, x):
            return load(field, s, x) if k == 1 else dst[s, x, full]

        span = planes(halo - k)
        prev = [get(s, span[0] - 1) for s in range(2)]
        cur = [get(s, span[0]) for s in range(2)]
        for x in span:
            at = part(x, halo - k)
            for s in range(2):
                nxt = get(s, x + 1)
                new = right[s, x, at] + MIX[s] * around(prev[s], cur[s], nxt, at)
                dst[s, x, OWN if k == halo else at] = new
                prev[s], cur[s] = cur[s], nxt


def sources(outs, nodes, first, rates, mixed):
    for out, step, halo in outs:
        thin = halo == 3
        load, own, full = (slim, FIRST, SLIM) if thin else (whole, OWN, slice(0, EXT))
        linear_w = [TABLE[step][j] - (1.0 if first + j == step + 1 else 0.0) for j in range(4)]
        react_w = [TABLE[step][j] - (1.0 if first + j == step else 0.0) for j in range(4)]
        total = sum(react_w)
        for x in planes(halo + 1):
            at = own if rows(x, halo + 1) == OWN else full
            us = [load(node, 0, x)[at] for node in nodes]
            vs = [load(node, 1, x)[at] for node in nodes]
            mix_u = sum(w * u for w, u in zip(linear_w, us))
            mix_v = sum(w * v for w, v in zip(linear_w, vs))
            mixed[0, x, at], mixed[1, x, at] = mix_u, mix_v
            if x in planes(halo):
                after, now = step + 1 - first, step - first
                sum_u = mix_u + (us[after] - us[now])
                sum_v = mix_v + (vs[after] - vs[now])
                uptake = sum(w * (u * v * v) for w, u, v in zip(react_w, us, vs))
                out[0, x, at] = 0.5 * (load(rates, 0, x)[at] * (total - sum_u) - uptake)
                out[1, x, at] = 0.5 * (uptake - load(rates, 1, x)[at] * sum_v)
        span = planes(halo)
        for s in range(2):
            prev, cur = mixed[s, span[0] - 1, full], mixed[s, span[0], full]
            for x in span:
                at = own if rows(x, halo) == OWN else full
                nxt = mixed[s, x + 1, full]
                new = out[s, x, at] + COEF[s] * (around(prev, cur, nxt, at) - 6.0 * cur[at])
                if thin:
                    out[s, x, OWN] = new[FIRST]
                    if at == full:
                        out[s, x, :BRICK] = out[s, x, 2 * BRICK :] = new[BRICK:]
                else:
                    out[s, x, at] = new
                prev, cur = cur, nxt


FULL = (1, 8, 7, None, None)
NEAR = (1, 4, 3, 4, 0)
RING_Y = (5, 8, 7, 0, 4)
RING_S = (4, 7, 6, 1, 3)


def tiles_y(kinds):
    return sum(2 if kind is FULL else 1 for kind in kinds)


def tiles_x(kind):
    return kind[1] - kind[0] + 1 + kind[2]


def four(first):
    index = row_index()
    return (index >= first) & (index < first + 4)


def even_y():
    return (lax.axis_index("level") + lax.axis_index("gy") // 2) % 2 == 0


def tiles_c(kinds):
    return sum(2 * (kind[1] - kind[0] + 1) for kind in kinds)


def pack_c(out, kinds, fields):
    at = 0
    for kind, field in zip(kinds, fields):
        for s in range(2):
            for e in range(kind[0], kind[1] + 1):
                out[at] = field[s, BRICK + e - 1, OWN]
                at += 1


def pack_y(outs, kinds, fields):
    *outs, centre = outs
    pack_c(centre, kinds, fields)
    even = even_y()
    at = 0
    for kind, field in zip(kinds, fields):
        if kind is not FULL:
            masks = [
                four(jnp.where(even, kind[3], kind[4])),
                four(jnp.where(even, kind[4], kind[3])),
            ]
        for i in range(BRICK):
            u, v = field[0, BRICK + i, OWN], field[1, BRICK + i, OWN]
            if kind is FULL:
                for out in outs:
                    out[at, i], out[at + 1, i] = u, v
            else:
                v = pltpu.roll(v, 4, 0)
                for out, mask in zip(outs, masks):
                    out[at, i] = jnp.where(mask, u, v)
        at += tiles_y([kind])


def widen(kinds, near, far, *refs):
    fields, refs = refs[: len(kinds)], refs[len(kinds) :]
    to_near, to_far, wide = (None, *refs) if len(refs) == 2 else (refs[3], None, refs[2])
    even = even_y()
    at = 0
    for f, (kind, field) in enumerate(zip(kinds, fields)):
        for i in range(BRICK):
            for s in range(2):
                tile = at + (s if kind is FULL else 0)
                a, b = near[tile, i], far[tile, i]
                low, high = jnp.where(even, b, a), jnp.where(even, a, b)
                if kind is not FULL and s == 1:
                    low, high = pltpu.roll(low, 4, 0), pltpu.roll(high, 4, 0)
                if kind in (RING_Y, RING_S):
                    low = jnp.where(four(kind[3]), low, field[s, BRICK + i, :BRICK])
                    high = jnp.where(four(kind[4]), high, field[s, BRICK + i, 2 * BRICK :])
                wide[2 * f + s, i, :BRICK] = low
                wide[2 * f + s, i, OWN] = field[s, BRICK + i, OWN]
                wide[2 * f + s, i, 2 * BRICK :] = high
        at += tiles_y([kind])
    pack_x(kinds, wide, to_near, to_far, True)


def pack_x(kinds, wide, to_near, to_far, ahead):
    index = row_index()
    at = late = 0
    for f, kind in enumerate(kinds):
        first, last, corners = kind[:3]
        for s in range(2):
            field = wide.at[2 * f + s]
            for out, plane, short in (
                (to_near, lambda e: BRICK - e, False),
                (to_far, lambda e: e - 1, ahead),
            ):
                if out is None:
                    continue
                start = late if short else at + last - first + 1
                if not short:
                    for e in range(first, last + 1):
                        out[at + e - first] = field[plane(e), OWN]
                for e in range(1, corners + 1):
                    low, other = (4, e) if kind is NEAR else (e + 7 - corners, corners + 1 - e)
                    out[start + e - 1] = jnp.where(
                        index >= low, field[plane(e), :BRICK], field[plane(other), 2 * BRICK :]
                    )
            at += tiles_x(kind)
            late += corners


def assemble(kinds, dsts, wide, near, far, centre=None, bases=()):
    bases = list(bases)
    at = late = ahead = 0
    for f, (kind, dst) in enumerate(zip(kinds, dsts)):
        first, last, corners = kind[:3]
        base = bases.pop(0) if kind in (RING_Y, RING_S) else None
        for s in range(2):
            for i in range(BRICK):
                dst[s, BRICK + i] = wide[2 * f + s, i]
            short = centre is not None
            for ref, own, first_at, start, plane in (
                (near, near, at, at + last - first + 1, lambda e: 2 * BRICK - 1 + e),
                (
                    far,
                    centre if short else far,
                    ahead if short else at,
                    late if short else at + last - first + 1,
                    lambda e: BRICK - e,
                ),
            ):
                for e in range(1, first):
                    dst[s, plane(e), OWN] = base[s, plane(e), OWN]
                for e in range(first, last + 1):
                    dst[s, plane(e), OWN] = own[first_at + e - first]
                for e in range(1, corners + 1):
                    other = e if kind is NEAR else corners + 1 - e
                    both = ref[start + e - 1]
                    dst[s, plane(e), :BRICK] = both
                    dst[s, plane(other), 2 * BRICK :] = both
            at += tiles_x(kind)
            ahead += last - first + 1
            late += corners


def pick(state, feed, kill, pair, brick, state_v, feed_v, kill_v, sems):
    p, far_p, far_q = first_sent(lax.axis_index("level"), lax.axis_index("gy") // 2)
    copies = [
        pltpu.make_async_copy(source, target, sems.at[i])
        for i, (source, target) in enumerate(((state, state_v), (feed, feed_v), (kill, kill_v)))
    ]
    for copy in copies:
        copy.start()
    for copy in copies:
        copy.wait()
    part = pl.ds(pl.multiple_of(far_q * BRICK, BRICK), BRICK)
    for f, field in enumerate((state_v.at[0], state_v.at[1], feed_v, kill_v)):
        for i in range(BRICK):
            pair[f, i] = field[p * BRICK + i]
            brick[f, i] = field[far_p * BRICK + i, part]


def widen_0(pair, far, wide, to_near, to_far):
    even = even_y()
    odd = odd_x()
    for f in range(4):
        for i in range(BRICK):
            at = jnp.where(odd == 0, i, BRICK - 1 - i)
            one, two, three = pair[f, at, :BRICK], pair[f, at, BRICK:], far[f, at]
            wide[f, i, :BRICK] = jnp.where(even, three, one)
            wide[f, i, OWN] = jnp.where(even, one, two)
            wide[f, i, 2 * BRICK :] = jnp.where(even, two, three)
    pack_x((FULL, FULL), wide, to_near, to_far, False)


KINDS = {
    0: (FULL, FULL),
    1: (FULL,),
    2: (FULL, RING_S, NEAR),
    3: (FULL, RING_Y, RING_S),
    4: (FULL, RING_S),
    5: (FULL, RING_S, NEAR),
    6: (NEAR,),
}


def round_0(wide, near, far, out, out_c, start, rates, y1, y2, right):
    assemble(KINDS[0], (start, rates), wide, near, far)
    for x in range(EXT):
        rates[1, x] = rates[0, x] + rates[1, x]
    advance(y1, start, rates, right, 8)
    advance(y2, y1, rates, right, 4)
    pack_y((out, out_c), KINDS[1], (y2,))


def round_1(wide, near, far, centre, start, rates, y1, out_a, out_b, out_c, y2, y3, z1, t, y4, s, right, mixed):
    assemble(KINDS[1], (y2,), wide, near, far, centre)
    advance(y3, y2, rates, right, 8)
    sources([(s, 0, 3), (t, 1, 3)], (start, y1, y2, y3), 0, rates, mixed)
    advance(z1, start, rates, right, 4, s)
    advance(y4, y3, rates, right, 4)
    pack_y((out_a, out_b, out_c), KINDS[2], (z1, t, y4))


def round_2(wide, near, far, centre, base, rates, y1, y2, y3, out_a, out_b, out_c, z1, z3, z2, s3, s1, y4, s2, right, mixed):
    assemble(KINDS[2], (z1, s1, y4), wide, near, far, centre, (base,))
    advance(z2, z1, rates, right, 8, s1)
    sources([(s2, 2, 3), (s3, 3, 3)], (y1, y2, y3, y4), 1, rates, mixed)
    advance(z3, z2, rates, right, 4, s2)
    pack_y((out_a, out_b, out_c), KINDS[3], (z3, z2, s3))


def round_3(
    wide, near, far, centre, base_y, base_s, start, rates, y1, out_a, out_b, out_c, y4, z1, z2, s2, s3, y2, y3, s, right, mixed
):
    assemble(KINDS[3], (y3, y2, s), wide, near, far, centre, (base_y, base_s))
    advance(y4, y3, rates, right, 8, s)
    sources([(s, 0, 7), (s3, 1, 3)], (start, y1, y2, y3), 0, rates, mixed)
    advance(z1, start, rates, right, 8, s)
    advance(z2, z1, rates, right, 4, s3)
    sources([(s2, 2, 3), (s3, 3, 3)], (y1, y2, y3, y4), 1, rates, mixed)
    pack_y((out_a, out_b, out_c), KINDS[4], (z2, s2))


def round_4(
    wide, near, far, centre, base, start, rates, y1, s3, out_a, out_b, out_c, y2, y3, z1, t, y4, s2, right, mixed
):
    assemble(KINDS[4], (y2, s2), wide, near, far, centre, (base,))
    advance(y3, y2, rates, right, 8, s2)
    sources([(s2, 0, 3), (t, 1, 3)], (start, y1, y2, y3), 0, rates, mixed)
    advance(z1, start, rates, right, 4, s2)
    advance(y4, y3, rates, right, 4, s3)
    pack_y((out_a, out_b, out_c), KINDS[5], (z1, t, y4))


def round_5(wide, near, far, centre, base, rates, y1, y2, y3, out_a, out_b, out_c, z3, s3, z1, s1, y4, z2, s2, right, mixed):
    assemble(KINDS[5], (z1, s1, y4), wide, near, far, centre, (base,))
    advance(z2, z1, rates, right, 8, s1)
    sources([(s2, 2, 3), (s3, 3, 3)], (y1, y2, y3, y4), 1, rates, mixed)
    advance(z3, z2, rates, right, 4, s2)
    pack_y((out_a, out_b, out_c), KINDS[6], (z3,))


def round_6(wide, near, far, centre, rates, s3, f0, f1, f2, keep, give, y3, y4, right, last):
    assemble(KINDS[6], (y3,), wide, near, far, centre)
    advance(y4, y3, rates, right, 4, s3)
    half = odd_x()
    for i in range(BRICK):
        x = jnp.where(half == 0, i, BRICK - 1 - i)
        for s in range(2):
            for level, field in enumerate((f0, f1, f2, y4)):
                last[level, s, x] = field[s, BRICK + i, OWN]
    for j in range(2):
        keep[j] = last[2 * half + j]
        give[j] = last[2 * (1 - half) + j]


def join(keep, got, out_0, out_1):
    half, odd = odd_x(), jnp.where(even_y(), 0, 1)
    for turn, out in enumerate((out_0, out_1)):
        j = jnp.where(odd == turn, 0, 1)
        for i in range(BRICK):
            for s in range(2):
                out[s, half * BRICK + i] = keep[j, s, i]
                out[s, (1 - half) * BRICK + i] = got[j, s, i]


def put(in_0, in_1, out, sems):
    odd = lax.axis_index("level") % 2
    copies = []
    for turn, piece in enumerate((in_0, in_1)):
        q = jnp.where(odd == turn, 0, 1)
        at = pl.ds(pl.multiple_of(q * BRICK, BRICK), BRICK)
        copies.append(pltpu.make_async_copy(piece, out.at[0, :, :, at], sems.at[turn]))
    for copy in copies:
        copy.start()
    for copy in copies:
        copy.wait()


def per_device(state, feed, kill):
    field = (2, EXT, EXT, LANES)
    block = (2, 2 * BRICK, 2 * BRICK, LANES)

    def brick(n):
        return (n, BRICK, BRICK, LANES)

    def sends(n):
        return [brick(tiles_y(KINDS[n]))] * 2 + [(tiles_c(KINDS[n]), BRICK, LANES)]

    def wide_shapes(n):
        count = len(KINDS[n])
        near = 2 * sum(tiles_x(kind) for kind in KINDS[n])
        far = 2 * sum(kind[2] for kind in KINDS[n]) if n else near
        return [(2 * count, BRICK, EXT, LANES), (near, BRICK, LANES), (far, BRICK, LANES)]

    def along_x(wide, to_near, to_far):
        return wide, sent(to_near, 0, False), sent(to_far, 0, True)

    def exchange(n, to_near, to_far, centre, *fields):
        got = sent(to_near, 1, False), sent(to_far, 1, True)
        centre = sent(centre, 0, True)
        kernel = functools.partial(widen, KINDS[n])
        wide, near, far = wide_shapes(n)
        to_far = call(kernel, f"corner_{n}", [far], (*got, *fields), [wide])[0]
        wide, to_near = call(kernel, f"widen_{n}", [wide, near], (*got, *fields, centre, to_far))
        return (*along_x(wide, to_near, to_far), centre)

    pair, one = call(
        pick,
        "pick",
        [(4, BRICK, 2 * BRICK, LANES), brick(4)],
        (state, feed, kill),
        [block, block[1:], block[1:], pltpu.SemaphoreType.DMA((3,))],
        space=HBM,
        limit=63,
    )
    pair = lax.ppermute(pair, AXES, spread_pairs(False))
    one = lax.ppermute(one, AXES, spread_pairs(True))
    wide = along_x(*call(widen_0, "widen_0", wide_shapes(0), (pair, one)))
    out, centre, start, rates, y1, y2 = call(
        round_0, "round_0", sends(1)[1:] + [field] * 4, wide, [field]
    )
    wide = exchange(1, out, out, centre, y2)
    *out, y2, y3, z1, t, final_0 = call(
        round_1, "round_1", sends(2) + [field] * 5, (*wide, start, rates, y1), [field] * 3
    )
    wide = exchange(2, *out, z1, t, final_0)
    *out, z1, z3, z2, s3 = call(
        round_2, "round_2", sends(3) + [field] * 4, (*wide, t, rates, y1, y2, y3), [field] * 5
    )
    wide = exchange(3, *out, z3, z2, s3)
    *out, final_1, y1, y2, s2, s4 = call(
        round_3, "round_3", sends(4) + [field] * 5, (*wide, z2, s3, start, rates, z1), [field] * 5
    )
    wide = exchange(4, *out, y2, s2)
    *out, y2, y3, z1, t, final_2 = call(
        round_4, "round_4", sends(5) + [field] * 5, (*wide, s2, start, rates, y1, s4), [field] * 3
    )
    wide = exchange(5, *out, z1, t, final_2)
    *out, z3, s3 = call(
        round_5, "round_5", sends(6) + [field] * 2, (*wide, t, rates, y1, y2, y3), [field] * 7
    )
    wide = exchange(6, *out, z3)
    keep, give = call(
        round_6,
        "round_6",
        [(2,) + brick(2)] * 2,
        (*wide, rates, s3, final_0, final_1, final_2),
        [field] * 3 + [(4,) + brick(2)],
    )
    half = (2, 2 * BRICK, BRICK, LANES)
    outs = call(join, "join", [half] * 2, (keep, sent(give, 0, False)))
    outs = [lax.ppermute(o, AXES, gather_pairs(turn)) for turn, o in enumerate(outs)]
    return call(
        put, "put", [(1,) + block], outs, [pltpu.SemaphoreType.DMA((2,))], out_space=HBM
    )[0]


def solution(mesh):
    return jax.shard_map(
        per_device,
        mesh=mesh,
        in_specs=(P(None, "gx", "gy", None), P("gx", "gy", None), P("gx", "gy", None)),
        out_specs=P("level", None, "gx", "gy", None),
        check_vma=False,
    )
```

```python
import functools

import jax
import jax.numpy as jnp
import numpy as np
from jax import lax
from jax.experimental import pallas as pl
from jax.experimental.pallas import tpu as pltpu
from jax.sharding import PartitionSpec as P


BRICK = 8
EXT = 3 * BRICK
LANES = 128
AXES = ("level", "gx", "gy")
COEF = (0.5, 0.25)
INV = tuple(1.0 / (1.0 + 6.0 * c) for c in COEF)
MIX = tuple(c / (1.0 + 6.0 * c) for c in COEF)
STEPS = 4
VMEM = pl.BlockSpec(memory_space=pltpu.VMEM)
HBM = pl.BlockSpec(memory_space=pltpu.HBM)


def quad_table(step_count):
    table_rows = []
    for n in range(step_count):
        first_node = min(max(n - 1, 0), step_count - 3)
        weights_row = []
        for j in range(4):
            coeffs = [1.0]
            for i in range(4):
                if i != j:
                    shifted = [0.0] + coeffs
                    scaled_terms = [-float(first_node + i) * c for c in coeffs] + [0.0]
                    coeffs = [
                        (shifted[k] + scaled_terms[k]) / float(j - i) for k in range(len(shifted))
                    ]
            integral = 0.0
            for k in range(len(coeffs)):
                integral = integral + coeffs[k] * ((n + 1.0) ** (k + 1) - float(n) ** (k + 1)) / (
                    k + 1.0
                )
            weights_row.append(float(np.float32(integral)))
        table_rows.append(weights_row)
    return table_rows


TABLE = quad_table(STEPS)


def linear(level, gx, gy):
    return (level * 8 + gx) * 8 + gy


WALK = (
    *((0, 0), (0, 1), (0, 2), (0, 3)),
    *((1, 3), (1, 2), (1, 1), (1, 0)),
    *((2, 0), (2, 1), (2, 2), (2, 3)),
    *((3, 3), (3, 2), (3, 1), (3, 0)),
)


def device_at(bx, by):
    (x, y), z = WALK[by], bx // 2
    core = (bx + (z % 4 != 3)) % 2
    return linear(y, (z // 2) * 2 + core, x * 2 + z % 2)


def odd_x():
    z = (lax.axis_index("gx") // 2) * 2 + lax.axis_index("gy") % 2
    return (lax.axis_index("gx") + jnp.where(z % 4 != 3, 1, 0)) % 2


def pairs_along(dim, odd):
    pairs = []
    for bx in range(16):
        for by in range(16):
            at = [bx, by]
            at[dim] = (at[dim] ^ 1) if not odd else (((at[dim] + 1) ^ 1) - 1) % 16
            pairs.append((device_at(bx, by), device_at(*at)))
    return pairs


def first_sent(level, x):
    return level // 2, level % 2, (level // 2 + x) % 2


def spread_pairs(beside):
    pairs = []
    for level in range(4):
        for gx in range(8):
            for gy in range(8):
                p, far_p, far_q = first_sent(level, gy // 2)
                bx, by = 2 * gx + p, 2 * gy + ((level + 1) // 2 + gy) % 2
                if beside:
                    bx, by = 2 * gx + far_p, (((2 * gy + far_q + 1) ^ 1) - 1) % 16
                pairs.append((linear(level, gx, gy), device_at(bx, by)))
    return pairs


def gather_pairs(turn):
    pairs = []
    for bx in range(16):
        for by in range(16):
            level = 2 * (bx % 2) + (turn ^ (by % 2))
            pairs.append((device_at(bx, by), linear(level, bx // 2, by // 2)))
    return pairs


def sent(array, dim, odd):
    return lax.ppermute(array, AXES, pairs_along(dim, odd))


def call(kernel, name, out_shapes, args, scratch=(), space=VMEM, out_space=VMEM, limit=40):
    return pl.pallas_call(
        kernel,
        name=name,
        out_shape=[jax.ShapeDtypeStruct(s, jnp.float32) for s in out_shapes],
        in_specs=[space] * len(args),
        out_specs=[out_space] * len(out_shapes),
        scratch_shapes=[s if not isinstance(s, tuple) else pltpu.VMEM(s, jnp.float32) for s in scratch],
        compiler_params=pltpu.CompilerParams(vmem_limit_bytes=limit << 20),
    )(*args)


def planes(halo):
    return range(BRICK - halo, 2 * BRICK + halo)


OWN = slice(BRICK, 2 * BRICK)


def rows(x, halo):
    away = max(BRICK - x, x - (2 * BRICK - 1), 0)
    return slice(0, EXT) if away < halo else OWN


def around(prev, cur, nxt, at):
    count = cur.shape[0]
    second = pltpu.roll(cur, 1, 0) + pltpu.roll(cur, count - 1, 0)
    third = pltpu.roll(cur[at], 1, 1) + pltpu.roll(cur[at], LANES - 1, 1)
    return (prev[at] + nxt[at]) + (second[at] + third)


FIRST, SLIM = slice(0, BRICK), slice(0, 2 * BRICK)


def slim(ref, s, x):
    return slimmed(ref[s, x])


def slimmed(cells):
    halo = jnp.where(row_index() < 4, cells[2 * BRICK :], cells[:BRICK])
    return jnp.concatenate([cells[OWN], halo], axis=0)


def row_index():
    return lax.broadcasted_iota(jnp.int32, (BRICK, LANES), 0)


def reacted(u, v, feed, both):
    uptake = u * v * v
    return 0.5 * (feed * (1.0 - u) - uptake), 0.5 * (uptake - both * v)


def whole(ref, s, x):
    return ref[s, x]


def advance(dst, field, rates, right, halo, source=None):
    thin = halo == 4
    load, own, full = (slim, FIRST, SLIM) if thin else (whole, OWN, slice(0, EXT))

    def part(x, halo):
        return own if rows(x, halo) == OWN else full

    for x in planes(halo - 1):
        at = part(x, halo - 1)
        u, v = load(field, 0, x)[at], load(field, 1, x)[at]
        du, dv = reacted(u, v, load(rates, 0, x)[at], load(rates, 1, x)[at])
        u, v = u + du, v + dv
        if source is not None:
            u, v = u + load(source, 0, x)[at], v + load(source, 1, x)[at]
        right[0, x, at] = INV[0] * u
        right[1, x, at] = INV[1] * v
    for k in range(1, 5):

        def get(s, x):
            return load(field, s, x) if k == 1 else dst[s, x, full]

        span = planes(halo - k)
        prev = [get(s, span[0] - 1) for s in range(2)]
        cur = [get(s, span[0]) for s in range(2)]
        for x in span:
            at = part(x, halo - k)
            for s in range(2):
                nxt = get(s, x + 1)
                if halo - k == 4 and at == full:
                    second = pltpu.roll(cur[s], 1, 0) + pltpu.roll(cur[s], EXT - 1, 0)
                    mid = slimmed(cur[s])
                    third = pltpu.roll(mid, 1, 1) + pltpu.roll(mid, LANES - 1, 1)
                    new = MIX[s] * (slimmed((prev[s] + nxt) + second) + third)
                    new = slimmed(right[s, x]) + new
                    dst[s, x, OWN] = new[FIRST]
                    dst[s, x, :BRICK] = dst[s, x, 2 * BRICK :] = new[BRICK:]
                else:
                    new = right[s, x, at] + MIX[s] * around(prev[s], cur[s], nxt, at)
                    dst[s, x, OWN if k == halo else at] = new
                prev[s], cur[s] = cur[s], nxt


def sources(outs, nodes, first, rates, mixed):
    for out, step, halo in outs:
        thin = halo == 3
        load, own, full = (slim, FIRST, SLIM) if thin else (whole, OWN, slice(0, EXT))
        linear_w = [TABLE[step][j] - (1.0 if first + j == step + 1 else 0.0) for j in range(4)]
        react_w = [TABLE[step][j] - (1.0 if first + j == step else 0.0) for j in range(4)]
        total = sum(react_w)
        for x in planes(halo + 1):
            at = own if rows(x, halo + 1) == OWN else full
            us = [load(node, 0, x)[at] for node in nodes]
            vs = [load(node, 1, x)[at] for node in nodes]
            mix_u = sum(w * u for w, u in zip(linear_w, us))
            mix_v = sum(w * v for w, v in zip(linear_w, vs))
            mixed[0, x, at], mixed[1, x, at] = mix_u, mix_v
            if x in planes(halo):
                after, now = step + 1 - first, step - first
                sum_u = mix_u + (us[after] - us[now])
                sum_v = mix_v + (vs[after] - vs[now])
                uptake = sum(w * (u * v * v) for w, u, v in zip(react_w, us, vs))
                out[0, x, at] = 0.5 * (load(rates, 0, x)[at] * (total - sum_u) - uptake)
                out[1, x, at] = 0.5 * (uptake - load(rates, 1, x)[at] * sum_v)
        span = planes(halo)
        for s in range(2):
            prev, cur = mixed[s, span[0] - 1, full], mixed[s, span[0], full]
            for x in span:
                at = own if rows(x, halo) == OWN else full
                nxt = mixed[s, x + 1, full]
                new = out[s, x, at] + COEF[s] * (around(prev, cur, nxt, at) - 6.0 * cur[at])
                if thin:
                    out[s, x, OWN] = new[FIRST]
                    if at == full:
                        out[s, x, :BRICK] = out[s, x, 2 * BRICK :] = new[BRICK:]
                else:
                    out[s, x, at] = new
                prev, cur = cur, nxt


FULL = (1, 8, 7, None, None)
NEAR = (1, 4, 3, 4, 0)
RING_Y = (5, 8, 7, 0, 4)
RING_S = (4, 7, 6, 1, 3)


def tiles_y(kinds):
    return sum(2 if kind is FULL else 1 for kind in kinds)


def tiles_x(kind):
    return kind[1] - kind[0] + 1 + kind[2]


def four(first):
    index = row_index()
    return (index >= first) & (index < first + 4)


def even_y():
    return (lax.axis_index("level") + lax.axis_index("gy") // 2) % 2 == 0


def tiles_c(kinds):
    return sum(2 * (kind[1] - kind[0] + 1) for kind in kinds)


def pack_c(out, kinds, fields):
    at = 0
    for kind, field in zip(kinds, fields):
        for s in range(2):
            for e in range(kind[0], kind[1] + 1):
                out[at] = field[s, BRICK + e - 1, OWN]
                at += 1


def pack_y(outs, kinds, fields):
    *outs, centre = outs
    pack_c(centre, kinds, fields)
    even = even_y()
    at = 0
    for kind, field in zip(kinds, fields):
        if kind is not FULL:
            masks = [
                four(jnp.where(even, kind[3], kind[4])),
                four(jnp.where(even, kind[4], kind[3])),
            ]
        for i in range(BRICK):
            u, v = field[0, BRICK + i, OWN], field[1, BRICK + i, OWN]
            if kind is FULL:
                for out in outs:
                    out[at, i], out[at + 1, i] = u, v
            else:
                v = pltpu.roll(v, 4, 0)
                for out, mask in zip(outs, masks):
                    out[at, i] = jnp.where(mask, u, v)
        at += tiles_y([kind])


def widen(kinds, near, far, *refs):
    fields, refs = refs[: len(kinds)], refs[len(kinds) :]
    to_near, to_far, wide = (None, *refs) if len(refs) == 2 else (refs[3], None, refs[2])
    even = even_y()
    at = 0
    for f, (kind, field) in enumerate(zip(kinds, fields)):
        for i in range(BRICK):
            for s in range(2):
                tile = at + (s if kind is FULL else 0)
                a, b = near[tile, i], far[tile, i]
                low, high = jnp.where(even, b, a), jnp.where(even, a, b)
                if kind is not FULL and s == 1:
                    low, high = pltpu.roll(low, 4, 0), pltpu.roll(high, 4, 0)
                if kind in (RING_Y, RING_S):
                    low = jnp.where(four(kind[3]), low, field[s, BRICK + i, :BRICK])
                    high = jnp.where(four(kind[4]), high, field[s, BRICK + i, 2 * BRICK :])
                wide[2 * f + s, i, :BRICK] = low
                wide[2 * f + s, i, OWN] = field[s, BRICK + i, OWN]
                wide[2 * f + s, i, 2 * BRICK :] = high
        at += tiles_y([kind])
    pack_x(kinds, wide, to_near, to_far, True)


def pack_x(kinds, wide, to_near, to_far, ahead):
    index = row_index()
    at = late = 0
    for f, kind in enumerate(kinds):
        first, last, corners = kind[:3]
        for s in range(2):
            field = wide.at[2 * f + s]
            for out, plane, short in (
                (to_near, lambda e: BRICK - e, False),
                (to_far, lambda e: e - 1, ahead),
            ):
                if out is None:
                    continue
                start = late if short else at + last - first + 1
                if not short:
                    for e in range(first, last + 1):
                        out[at + e - first] = field[plane(e), OWN]
                for e in range(1, corners + 1):
                    low, other = (4, e) if kind is NEAR else (e + 7 - corners, corners + 1 - e)
                    out[start + e - 1] = jnp.where(
                        index >= low, field[plane(e), :BRICK], field[plane(other), 2 * BRICK :]
                    )
            at += tiles_x(kind)
            late += corners


def assemble(kinds, dsts, wide, near, far, centre=None, bases=()):
    bases = list(bases)
    at = late = ahead = 0
    for f, (kind, dst) in enumerate(zip(kinds, dsts)):
        first, last, corners = kind[:3]
        base = bases.pop(0) if kind in (RING_Y, RING_S) else None
        for s in range(2):
            for i in range(BRICK):
                dst[s, BRICK + i] = wide[2 * f + s, i]
            short = centre is not None
            for ref, own, first_at, start, plane in (
                (near, near, at, at + last - first + 1, lambda e: 2 * BRICK - 1 + e),
                (
                    far,
                    centre if short else far,
                    ahead if short else at,
                    late if short else at + last - first + 1,
                    lambda e: BRICK - e,
                ),
            ):
                for e in range(1, first):
                    dst[s, plane(e), OWN] = base[s, plane(e), OWN]
                for e in range(first, last + 1):
                    dst[s, plane(e), OWN] = own[first_at + e - first]
                for e in range(1, corners + 1):
                    other = e if kind is NEAR else corners + 1 - e
                    both = ref[start + e - 1]
                    dst[s, plane(e), :BRICK] = both
                    dst[s, plane(other), 2 * BRICK :] = both
            at += tiles_x(kind)
            ahead += last - first + 1
            late += corners


def pick(state, feed, kill, pair, brick, state_v, feed_v, kill_v, sems):
    p, far_p, far_q = first_sent(lax.axis_index("level"), lax.axis_index("gy") // 2)
    copies = [
        pltpu.make_async_copy(source, target, sems.at[i])
        for i, (source, target) in enumerate(((state, state_v), (feed, feed_v), (kill, kill_v)))
    ]
    for copy in copies:
        copy.start()
    for copy in copies:
        copy.wait()
    part = pl.ds(pl.multiple_of(far_q * BRICK, BRICK), BRICK)
    for f, field in enumerate((state_v.at[0], state_v.at[1], feed_v, kill_v)):
        for i in range(BRICK):
            pair[f, i] = field[p * BRICK + i]
            brick[f, i] = field[far_p * BRICK + i, part]


def widen_0(pair, far, wide, to_near, to_far):
    even = even_y()
    odd = odd_x()
    for f in range(4):
        for i in range(BRICK):
            at = jnp.where(odd == 0, i, BRICK - 1 - i)
            one, two, three = pair[f, at, :BRICK], pair[f, at, BRICK:], far[f, at]
            wide[f, i, :BRICK] = jnp.where(even, three, one)
            wide[f, i, OWN] = jnp.where(even, one, two)
            wide[f, i, 2 * BRICK :] = jnp.where(even, two, three)
    pack_x((FULL, FULL), wide, to_near, to_far, False)


KINDS = {
    0: (FULL, FULL),
    1: (FULL,),
    2: (FULL, RING_S, NEAR),
    3: (FULL, RING_Y, RING_S),
    4: (FULL, RING_S),
    5: (FULL, RING_S, NEAR),
    6: (NEAR,),
}


def round_0(wide, near, far, out, out_c, start, rates, y1, y2, right):
    assemble(KINDS[0], (start, rates), wide, near, far)
    for x in range(EXT):
        rates[1, x] = rates[0, x] + rates[1, x]
    advance(y1, start, rates, right, 8)
    advance(y2, y1, rates, right, 4)
    pack_y((out, out_c), KINDS[1], (y2,))


def round_1(wide, near, far, centre, start, rates, y1, out_a, out_b, out_c, y2, y3, z1, t, y4, s, right, mixed):
    assemble(KINDS[1], (y2,), wide, near, far, centre)
    advance(y3, y2, rates, right, 8)
    sources([(s, 0, 3), (t, 1, 3)], (start, y1, y2, y3), 0, rates, mixed)
    advance(z1, start, rates, right, 4, s)
    advance(y4, y3, rates, right, 4)
    pack_y((out_a, out_b, out_c), KINDS[2], (z1, t, y4))


def round_2(wide, near, far, centre, base, rates, y1, y2, y3, out_a, out_b, out_c, z1, z3, z2, s3, s1, y4, s2, right, mixed):
    assemble(KINDS[2], (z1, s1, y4), wide, near, far, centre, (base,))
    advance(z2, z1, rates, right, 8, s1)
    sources([(s2, 2, 3), (s3, 3, 3)], (y1, y2, y3, y4), 1, rates, mixed)
    advance(z3, z2, rates, right, 4, s2)
    pack_y((out_a, out_b, out_c), KINDS[3], (z3, z2, s3))


def round_3(
    wide, near, far, centre, base_y, base_s, start, rates, y1, out_a, out_b, out_c, y4, z1, z2, s2, s3, y2, y3, s, right, mixed
):
    assemble(KINDS[3], (y3, y2, s), wide, near, far, centre, (base_y, base_s))
    advance(y4, y3, rates, right, 8, s)
    sources([(s, 0, 7), (s3, 1, 3)], (start, y1, y2, y3), 0, rates, mixed)
    advance(z1, start, rates, right, 8, s)
    advance(z2, z1, rates, right, 4, s3)
    sources([(s2, 2, 3), (s3, 3, 3)], (y1, y2, y3, y4), 1, rates, mixed)
    pack_y((out_a, out_b, out_c), KINDS[4], (z2, s2))


def round_4(
    wide, near, far, centre, base, start, rates, y1, s3, out_a, out_b, out_c, y2, y3, z1, t, y4, s2, right, mixed
):
    assemble(KINDS[4], (y2, s2), wide, near, far, centre, (base,))
    advance(y3, y2, rates, right, 8, s2)
    sources([(s2, 0, 3), (t, 1, 3)], (start, y1, y2, y3), 0, rates, mixed)
    advance(z1, start, rates, right, 4, s2)
    advance(y4, y3, rates, right, 4, s3)
    pack_y((out_a, out_b, out_c), KINDS[5], (z1, t, y4))


def round_5(wide, near, far, centre, base, rates, y1, y2, y3, out_a, out_b, out_c, z3, s3, z1, s1, y4, z2, s2, right, mixed):
    assemble(KINDS[5], (z1, s1, y4), wide, near, far, centre, (base,))
    advance(z2, z1, rates, right, 8, s1)
    sources([(s2, 2, 3), (s3, 3, 3)], (y1, y2, y3, y4), 1, rates, mixed)
    advance(z3, z2, rates, right, 4, s2)
    pack_y((out_a, out_b, out_c), KINDS[6], (z3,))


def round_6(wide, near, far, centre, rates, s3, f0, f1, f2, keep, give, y3, y4, right, last):
    assemble(KINDS[6], (y3,), wide, near, far, centre)
    advance(y4, y3, rates, right, 4, s3)
    half = odd_x()
    for i in range(BRICK):
        x = jnp.where(half == 0, i, BRICK - 1 - i)
        for s in range(2):
            for level, field in enumerate((f0, f1, f2, y4)):
                last[level, s, x] = field[s, BRICK + i, OWN]
    for j in range(2):
        keep[j] = last[2 * half + j]
        give[j] = last[2 * (1 - half) + j]


def join(keep, got, out_0, out_1):
    half, odd = odd_x(), jnp.where(even_y(), 0, 1)
    for turn, out in enumerate((out_0, out_1)):
        j = jnp.where(odd == turn, 0, 1)
        for i in range(BRICK):
            for s in range(2):
                out[s, half * BRICK + i] = keep[j, s, i]
                out[s, (1 - half) * BRICK + i] = got[j, s, i]


def put(in_0, in_1, out, sems):
    odd = lax.axis_index("level") % 2
    copies = []
    for turn, piece in enumerate((in_0, in_1)):
        q = jnp.where(odd == turn, 0, 1)
        at = pl.ds(pl.multiple_of(q * BRICK, BRICK), BRICK)
        copies.append(pltpu.make_async_copy(piece, out.at[0, :, :, at], sems.at[turn]))
    for copy in copies:
        copy.start()
    for copy in copies:
        copy.wait()


def per_device(state, feed, kill):
    field = (2, EXT, EXT, LANES)
    block = (2, 2 * BRICK, 2 * BRICK, LANES)

    def brick(n):
        return (n, BRICK, BRICK, LANES)

    def sends(n):
        return [brick(tiles_y(KINDS[n]))] * 2 + [(tiles_c(KINDS[n]), BRICK, LANES)]

    def wide_shapes(n):
        count = len(KINDS[n])
        near = 2 * sum(tiles_x(kind) for kind in KINDS[n])
        far = 2 * sum(kind[2] for kind in KINDS[n]) if n else near
        return [(2 * count, BRICK, EXT, LANES), (near, BRICK, LANES), (far, BRICK, LANES)]

    def along_x(wide, to_near, to_far):
        return wide, sent(to_near, 0, False), sent(to_far, 0, True)

    def exchange(n, to_near, to_far, centre, *fields):
        got = sent(to_near, 1, False), sent(to_far, 1, True)
        centre = sent(centre, 0, True)
        kernel = functools.partial(widen, KINDS[n])
        wide, near, far = wide_shapes(n)
        to_far = call(kernel, f"corner_{n}", [far], (*got, *fields), [wide])[0]
        wide, to_near = call(kernel, f"widen_{n}", [wide, near], (*got, *fields, centre, to_far))
        return (*along_x(wide, to_near, to_far), centre)

    pair, one = call(
        pick,
        "pick",
        [(4, BRICK, 2 * BRICK, LANES), brick(4)],
        (state, feed, kill),
        [block, block[1:], block[1:], pltpu.SemaphoreType.DMA((3,))],
        space=HBM,
        limit=63,
    )
    pair = lax.ppermute(pair, AXES, spread_pairs(False))
    one = lax.ppermute(one, AXES, spread_pairs(True))
    wide = along_x(*call(widen_0, "widen_0", wide_shapes(0), (pair, one)))
    out, centre, start, rates, y1, y2 = call(
        round_0, "round_0", sends(1)[1:] + [field] * 4, wide, [field]
    )
    wide = exchange(1, out, out, centre, y2)
    *out, y2, y3, z1, t, final_0 = call(
        round_1, "round_1", sends(2) + [field] * 5, (*wide, start, rates, y1), [field] * 3
    )
    wide = exchange(2, *out, z1, t, final_0)
    *out, z1, z3, z2, s3 = call(
        round_2, "round_2", sends(3) + [field] * 4, (*wide, t, rates, y1, y2, y3), [field] * 5
    )
    wide = exchange(3, *out, z3, z2, s3)
    *out, final_1, y1, y2, s2, s4 = call(
        round_3, "round_3", sends(4) + [field] * 5, (*wide, z2, s3, start, rates, z1), [field] * 5
    )
    wide = exchange(4, *out, y2, s2)
    *out, y2, y3, z1, t, final_2 = call(
        round_4, "round_4", sends(5) + [field] * 5, (*wide, s2, start, rates, y1, s4), [field] * 3
    )
    wide = exchange(5, *out, z1, t, final_2)
    *out, z3, s3 = call(
        round_5, "round_5", sends(6) + [field] * 2, (*wide, t, rates, y1, y2, y3), [field] * 7
    )
    wide = exchange(6, *out, z3)
    keep, give = call(
        round_6,
        "round_6",
        [(2,) + brick(2)] * 2,
        (*wide, rates, s3, final_0, final_1, final_2),
        [field] * 3 + [(4,) + brick(2)],
    )
    half = (2, 2 * BRICK, BRICK, LANES)
    outs = call(join, "join", [half] * 2, (keep, sent(give, 0, False)))
    outs = [lax.ppermute(o, AXES, gather_pairs(turn)) for turn, o in enumerate(outs)]
    return call(
        put, "put", [(1,) + block], outs, [pltpu.SemaphoreType.DMA((2,))], out_space=HBM
    )[0]


def solution(mesh):
    return jax.shard_map(
        per_device,
        mesh=mesh,
        in_specs=(P(None, "gx", "gy", None), P("gx", "gy", None), P("gx", "gy", None)),
        out_specs=P("level", None, "gx", "gy", None),
        check_vma=False,
    )
```
